32 devices in a mesh: groups: 2 (over y), ep: 4 (over z), sub: 2 (over x), tp: 2 (over core).
Axes of the slice: x: 2, y: 2, z: 4, core: 2. Of those that a mesh axis runs over, the one named last changes fastest.
Arguments:
- rows: bfloat16 [1024, 4096], P(('groups', 'ep'), ('sub', 'tp')), parts along dimension 0, may hold values from -6 to 6
- path: int32 [4, 1024, 1], P(None, ('groups', 'ep')), parts along dimension 1, may hold values from 0 to 7; in each aligned block of 128 rows (0 to 127, 128 to 255, ..., all dimensions but the last counted through in order) at most 32 rows name the same one
- norm_gain: float32 [8, 4096], P(('ep', 'tp')), may hold values from 0.1 to 1.9
- gate_weight: bfloat16 [8, 1408, 4096], P(('ep', 'tp'), 'sub'), may hold values from -0.09375 to 0.09375
- up_weight: bfloat16 [8, 1408, 4096], P(('ep', 'tp'), 'sub'), may hold values from -0.09375 to 0.09375
- down_weight: bfloat16 [8, 1408, 4096], P(('ep', 'tp'), 'sub'), may hold values from -0.15625 to 0.15625
Outputs:
- chained: bfloat16 [1024, 4096], P(('groups', 'ep'), ('sub', 'tp')), parts along dimension 0
The draws below stay inside these ranges and needn't reach their ends.
There are 2 independent parts, one for each index of `groups`. The reference program is written for one: setup_inputs(seed, part) draws one part's arguments, and reference() takes and returns one part's arrays. A program takes and returns all parts, laid end to end along the dimension named above; an argument that names none is the same for every part. Nothing has to cross between parts.
Inputs may be any that keep to these rules, and one draw needn't show every extreme that they name: `path`: in each aligned block of 128 rows of one hop no expert is named by more than 32 rows, and in some blocks one expert is named by exactly 32.
All inputs are finite; a program needn't handle non-finite values.
Results may differ from the reference program's by a relative error of at most 0.02.
Values may be sent and summed in bfloat16 or wider, within the bound.
A program may use at most 64 MiB of HBM per device.

```python
import math
import jax
import jax.numpy as jnp
import numpy as np
from jax import lax

D = 4096
HID = 1408
HOPS = 4
ROWS_EP = 128
EXPERTS = 8
ROWS = 512
CAP = 32
HID_PARTS = 2


def block_scale(stream_key, dims, cuts, smallest, largest):
    level, own = 1.0, jax.random.fold_in(stream_key, 6)
    for position, parts in cuts:
        draws = jnp.exp(jax.random.uniform(jax.random.fold_in(own, position), (parts,), jnp.float32, smallest / len(cuts), largest / len(cuts)))
        level = level * jnp.repeat(draws, dims[position] // parts).reshape([-1 if axis == position else 1 for axis in range(len(dims))])
    return level


def shared_out(stream_key, own, number, rows, amount, top, most, lean):
    order = jax.random.permutation(stream_key, amount)
    crowded, common = portions_of(amount, rows * top, most, lean, True), portions_of(amount, rows * top, most, lean, False)
    places = jnp.arange(amount)

    def named(sizes, turn):
        used = int((sizes > 0).sum())
        fixed = max(1, used // 4)
        moved = fixed + (places - fixed + turn * (used - fixed)) % max(1, amount - fixed)
        return jnp.zeros((amount,), jnp.int32).at[order[jnp.where(places < fixed, places, moved)]].set(jnp.asarray(sizes, jnp.int32))

    sizes = jnp.where(number % 4 == 0, named(crowded, number // 4), named(common, number - number // 4 - 1))
    mixed = jax.random.permutation(jax.random.fold_in(own, 3), amount)
    source_of, receiver = mixed[0:amount // 2 * 2:2], mixed[1:amount // 2 * 2:2]
    room = jnp.minimum(sizes[source_of] - 1, most - sizes[receiver]) // 2
    room = jnp.where((source_of == order[0]) | (receiver == order[0]) | (sizes[receiver] == 0), 0, jnp.maximum(room, 0))
    moved = jax.random.randint(jax.random.fold_in(own, 4), (amount // 2,), 0, 1 << 20) % (room + 1)
    sizes = sizes.at[source_of].add(-moved).at[receiver].add(moved)
    items = jnp.searchsorted(jnp.cumsum(sizes), jnp.arange(rows * top), side="right").astype(jnp.int32)
    grid = items.reshape(top, rows).T
    grid = grid[jax.random.permutation(jax.random.fold_in(own, 1), rows)]
    turn = jax.random.randint(jax.random.fold_in(own, 2), (rows, 1), 0, top)
    return jnp.take_along_axis(grid, (jnp.arange(top)[None, :] + turn) % top, axis=1)


def portions_of(count, total, limit, skew, full):
    loads = [(1 << 20) // math.isqrt(rank ** skew) + 1 for rank in range(1, count + 1)]
    largest = limit if full else min(limit, max(-(-total // count), total * loads[0] // sum(loads)))
    least = 1 if total - largest >= count - 1 else 0
    holding, spare = [largest] + [least] * (count - 1), total - largest - least * (count - 1)
    while spare > 0:
        candidates = [i for i in range(1, count) if holding[i] < largest] or [i for i in range(1, count) if holding[i] < limit]
        pool, left = sum([loads[i] for i in candidates]), spare
        for i in candidates:
            extra = min(limit - holding[i], max(1, left * loads[i] // pool), spare)
            holding[i] = holding[i] + extra
            spare = spare - extra
    return np.array(holding)


def centred(rng, extent, deviation, most, shards=(), held_as=jnp.bfloat16):
    factor_of = block_scale(rng, extent, shards, -0.22, 0.18) if shards else 1.0
    entries = jax.random.normal(rng, extent, jnp.float32) * deviation * factor_of
    return jnp.minimum(jnp.maximum(entries, -most), most).astype(held_as)


def setup_inputs(seed: int = 0, part: int = 0) -> dict:
    arg_keys = jax.random.split(jax.random.key(seed), 7)
    part_splits = jax.random.split(jax.random.fold_in(arg_keys[6], part), 7)
    rows = centred(part_splits[0], (ROWS, D), 1.0, 6.0, ((0, 4), (1, 4)))
    path_keys = jax.random.split(jax.random.fold_in(part_splits[1], 1), HOPS * ROWS // ROWS_EP)
    path_turns = jax.random.permutation(jax.random.fold_in(part_splits[1], 3), HOPS * ROWS // ROWS_EP)
    path = jax.vmap(lambda own, number: shared_out(jax.random.fold_in(part_splits[1], 2), own, number, ROWS_EP, EXPERTS, 1, CAP, 2))(path_keys, path_turns).reshape((HOPS, ROWS, 1))
    norm_gain = jnp.clip(1.0 + 0.18 * jax.random.normal(arg_keys[2], (EXPERTS, D), jnp.float32), 0.1, 1.9)
    gate_weight = centred(arg_keys[3], (EXPERTS, HID, D), D ** -0.5, 0.09375, ((0, 8), (1, 2)))
    up_weight = centred(arg_keys[4], (EXPERTS, HID, D), D ** -0.5, 0.09375, ((0, 8), (1, 2)))
    down_weight = centred(arg_keys[5], (EXPERTS, HID, D), HID ** -0.5, 0.15625, ((0, 8), (1, 2)))
    return dict(rows=rows, path=path, norm_gain=norm_gain, gate_weight=gate_weight, up_weight=up_weight, down_weight=down_weight)


EPS = 1e-06

def one_expert(pieces):
    inputs, gain, gate_w, up_w, down_w = pieces
    values = inputs.astype(jnp.float32)
    meansq = lax.optimization_barrier(jnp.mean(values * values, axis=-1, keepdims=True))
    normed = (values * lax.rsqrt(meansq + EPS) * gain[None, :]).astype(jnp.bfloat16)
    gate = lax.dot_general(normed, gate_w, (((1,), (1,)), ((), ())), preferred_element_type=jnp.float32)
    upward = lax.dot_general(normed, up_w, (((1,), (1,)), ((), ())), preferred_element_type=jnp.float32)
    hidden = (jax.nn.silu(gate) * upward).astype(jnp.bfloat16)
    width = HID // HID_PARTS
    blocked = hidden.reshape(hidden.shape[0], HID_PARTS, width).astype(jnp.float32)
    downs = down_w.reshape(HID_PARTS, width, D).astype(jnp.float32)
    partials = jnp.einsum('rkh,khd->krd', blocked, downs).astype(jnp.bfloat16)
    partials = lax.optimization_barrier(partials).astype(jnp.float32)
    return lax.optimization_barrier(jnp.sum(partials, axis=0)).astype(jnp.bfloat16)

def hop_update(state, routing, norm_gain, gate_weight, up_weight, down_weight):
    blocks = state.shape[0] // ROWS_EP
    grouped = routing.reshape(blocks, ROWS_EP).astype(jnp.int32)
    onehot = (grouped[:, :, None] == jnp.arange(EXPERTS, dtype=jnp.int32)[None, None, :]).astype(jnp.int32)
    rank_in = lax.optimization_barrier(jnp.sum((jnp.cumsum(onehot, axis=1) - onehot) * onehot, axis=2)).astype(jnp.int32)
    block_index = jnp.arange(blocks, dtype=jnp.int32)[:, None]
    target = ((grouped * blocks + block_index) * CAP + rank_in).reshape(-1).astype(jnp.int32)
    buffer = jnp.zeros((EXPERTS * blocks * CAP, D), jnp.bfloat16).at[target].set(state)
    buffer = buffer.reshape(EXPERTS, blocks * CAP, D)
    updates = lax.map(one_expert, (buffer, norm_gain, gate_weight, up_weight, down_weight))
    update = updates.reshape(EXPERTS * blocks * CAP, D)[target]
    update = lax.optimization_barrier(update)
    return (state.astype(jnp.float32) + update.astype(jnp.float32)).astype(jnp.bfloat16)

def reference(rows, path, norm_gain, gate_weight, up_weight, down_weight):
    state = rows
    for hop_index in range(HOPS):
        state = hop_update(state, path[hop_index, :, 0], norm_gain, gate_weight, up_weight, down_weight)
    return state
```

```python
import functools

import jax
import jax.numpy as jnp
from jax import lax
from jax.experimental import pallas as pl
from jax.experimental.pallas import tpu as pltpu
from jax.sharding import PartitionSpec as P

EPS = 1e-06
MESH = pl.DeviceIdType.MESH
F32 = jnp.float32
BF16 = jnp.bfloat16


def partner(index, distance, count):
    out, bit = 0, 1
    while bit < count:
        own = (index // bit) % 2
        out = out + bit * ((1 - own) if (distance // bit) % 2 else own)
        bit *= 2
    return out


def chain_kernel(
    sizes,
    rows_ref,
    path_ref,
    gain_ref,
    gate_hbm,
    up_hbm,
    down_hbm,
    state_ref,
    gate_ref,
    up_ref,
    down_ref,
    placing_ref,
    packed_ref,
    arrived_ref,
    normed_ref,
    hidden_ref,
    part_out_ref,
    part_in_ref,
    own_ref,
    summed_ref,
    returned_ref,
    load_sem,
    disp_send,
    disp_recv,
    fwd_send,
    fwd_recv,
    part_send,
    part_recv,
    ret_send,
    ret_recv,
):
    ep, tp, sub, cap, per_chunk = sizes
    z, s, t = lax.axis_index("ep"), lax.axis_index("sub"), lax.axis_index("tp")
    hops = path_ref.shape[0]
    local_rows, quarter = state_ref.shape
    half = quarter * tp
    experts = ep * tp
    chunks = ep // per_chunk
    chunk_rows = per_chunk * cap
    here = s * tp + t

    loads = [
        pltpu.make_async_copy(src, dst, load_sem.at[i])
        for i, (src, dst) in enumerate(
            ((gate_hbm, gate_ref), (up_hbm, up_ref), (down_hbm, down_ref))
        )
    ]
    for load in loads:
        load.start()

    barrier = pltpu.get_barrier_semaphore()
    peers = 0
    for k in range(ep):
        for c in range(tp):
            if k or c:
                pl.semaphore_signal(
                    barrier, inc=1,
                    device_id={"ep": partner(z, k, ep), "tp": (t + c) % tp},
                    device_id_type=MESH,
                )
                peers += 1
    for j in range(1, sub):
        pl.semaphore_signal(
            barrier, inc=1, device_id={"sub": (s + j) % sub}, device_id_type=MESH
        )
        peers += 1

    def rows_of(k):
        return pl.ds(k * cap, cap)

    def rows_in(chunk):
        return pl.ds(chunk * chunk_rows, chunk_rows)

    def dispatch_copy(k, c):
        to_z, to_t = partner(z, k, ep), (t + c) % tp
        return pltpu.make_async_remote_copy(
            src_ref=packed_ref.at[to_z * tp + to_t],
            dst_ref=arrived_ref.at[here, rows_of(k)],
            send_sem=disp_send.at[k, c],
            recv_sem=disp_recv.at[k, c],
            device_id={"ep": to_z, "tp": to_t},
            device_id_type=MESH,
        )

    def forward_copy(k, j):
        block = arrived_ref.at[pl.ds(s * tp, tp), rows_of(k)]
        return pltpu.make_async_remote_copy(
            src_ref=block,
            dst_ref=block,
            send_sem=fwd_send.at[k, j - 1],
            recv_sem=fwd_recv.at[k, j - 1],
            device_id={"sub": (s + j) % sub},
            device_id_type=MESH,
        )

    def part_copy(chunk, j):
        return pltpu.make_async_remote_copy(
            src_ref=part_out_ref.at[j - 1, rows_in(chunk)],
            dst_ref=part_in_ref.at[j - 1, rows_in(chunk)],
            send_sem=part_send.at[chunk, j - 1],
            recv_sem=part_recv.at[chunk, j - 1],
            device_id={"sub": (s + j) % sub},
            device_id_type=MESH,
        )

    def return_copy(k, c):
        to_z, to_t = partner(z, k, ep), (t + c) % tp
        return pltpu.make_async_remote_copy(
            src_ref=summed_ref.at[to_t, rows_of(k)],
            dst_ref=returned_ref.at[z * tp + t],
            send_sem=ret_send.at[k, c],
            recv_sem=ret_recv.at[k, c],
            device_id={"ep": to_z, "tp": to_t},
            device_id_type=MESH,
        )

    remote = [(k, c) for k in range(ep) for c in range(tp) if k or c]

    def make_placing(hop):
        named = path_ref[pl.ds(hop, 1), :]
        lines = -(-experts // 8) * 8
        onehot = (
            lax.broadcasted_iota(jnp.int32, (lines, local_rows), 0) == named
        ).astype(F32)
        earlier = (
            lax.broadcasted_iota(jnp.int32, (local_rows, local_rows), 0)
            < lax.broadcasted_iota(jnp.int32, (local_rows, local_rows), 1)
        ).astype(F32)
        before = jnp.dot(
            onehot.astype(BF16), earlier.astype(BF16), preferred_element_type=F32
        )
        rank = jnp.sum(before * onehot, axis=0, keepdims=True)
        target = named.astype(F32) * float(cap) + rank
        slots = lax.broadcasted_iota(jnp.int32, (experts * cap, local_rows), 0)
        placing_ref[hop] = jnp.where(slots.astype(F32) == target, 1.0, 0.0).astype(BF16)

    def dispatch(hop):
        packed = jnp.dot(
            placing_ref[hop], state_ref[...], preferred_element_type=F32
        ).astype(BF16)
        packed_ref[...] = packed.reshape(experts, cap, quarter)
        for k, c in remote:
            dispatch_copy(k, c).start()
        arrived_ref[here, rows_of(0), :] = packed_ref[z * tp + t]

    def forward(k):
        for c in range(tp):
            if k or c:
                dispatch_copy(k, c).wait_recv()
        for j in range(1, sub):
            forward_copy(k, j).start()

    def normalise(k):
        for j in range(1, sub):
            forward_copy(k, j).wait_recv()
        total = jnp.zeros((cap, 1), F32)
        for q in range(sub * tp):
            value = arrived_ref[q, rows_of(k), :].astype(F32)
            total = total + jnp.sum(value * value, axis=-1, keepdims=True)
        scale = lax.rsqrt(total / float(quarter * sub * tp) + EPS)
        for q in range(sub * tp):
            value = arrived_ref[q, rows_of(k), :].astype(F32)
            columns = pl.ds(q * quarter, quarter)
            normed_ref[rows_of(k), columns] = (
                value * scale * gain_ref[:, columns]
            ).astype(BF16)

    def expand(chunk):
        for k in range(chunk * per_chunk, (chunk + 1) * per_chunk):
            normalise(k)
        normed = normed_ref[rows_in(chunk), :]
        dims = (((1,), (1,)), ((), ()))
        gate = lax.dot_general(normed, gate_ref[0], dims, preferred_element_type=F32)
        upward = lax.dot_general(normed, up_ref[0], dims, preferred_element_type=F32)
        hidden_ref[rows_in(chunk), :] = (
            gate / (1.0 + jnp.exp(-gate)) * upward
        ).astype(BF16)

    tile = min(512, half)

    def contract(chunk, j, out):
        base = ((s + j) % sub) * half

        def step(i, carry):
            inside = pl.ds(pl.multiple_of(i * tile, tile), tile)
            columns = pl.ds(pl.multiple_of(base + i * tile, tile), tile)
            out[rows_in(chunk), inside] = jnp.dot(
                hidden_ref[rows_in(chunk), :],
                down_ref[0, :, columns],
                preferred_element_type=F32,
            ).astype(out.dtype)
            return carry

        lax.fori_loop(0, half // tile, step, 0)

    def project(chunk):
        for j in range(1, sub):
            contract(chunk, j, part_out_ref.at[j - 1])
            part_copy(chunk, j).start()
        contract(chunk, 0, own_ref)

    def give_back(chunk):
        for j in range(1, sub):
            part_copy(chunk, j).wait_recv()
        for k in range(chunk * per_chunk, (chunk + 1) * per_chunk):
            for i in range(tp):
                columns = pl.ds(i * quarter, quarter)
                value = own_ref[rows_of(k), columns]
                for j in range(1, sub):
                    value = value + part_in_ref[j - 1, rows_of(k), columns].astype(F32)
                summed_ref[i, rows_of(k), :] = value.astype(BF16)
            for c in range(tp):
                if k or c:
                    return_copy(k, c).start()
                else:
                    returned_ref[z * tp + t] = summed_ref[t, rows_of(k), :]

    state_ref[...] = rows_ref[...]
    make_placing(0)
    pl.semaphore_wait(barrier, peers)
    dispatch(0)
    for hop in range(1, hops):
        make_placing(hop)
    for load in loads:
        load.wait()

    def one_hop(hop, carry):
        for k in range(per_chunk):
            forward(k)
        expand(0)
        for k in range(per_chunk, ep):
            forward(k)
        project(0)
        for chunk in range(1, chunks):
            expand(chunk)
            project(chunk)
        for k, c in remote:
            dispatch_copy(k, c).wait_send()
        for k in range(ep):
            for j in range(1, sub):
                forward_copy(k, j).wait_send()
        for chunk in range(chunks):
            give_back(chunk)
        for chunk in range(chunks):
            for j in range(1, sub):
                part_copy(chunk, j).wait_send()
        for k, c in remote:
            return_copy(k, c).wait_recv()
        update = lax.dot_general(
            placing_ref[hop],
            returned_ref[...].reshape(experts * cap, quarter),
            (((0,), (0,)), ((), ())),
            preferred_element_type=F32,
        )
        state_ref[...] = (state_ref[...].astype(F32) + update).astype(BF16)

        @pl.when(hop < hops - 1)
        def _():
            dispatch(hop + 1)

        for k, c in remote:
            return_copy(k, c).wait_send()
        return carry

    lax.fori_loop(0, hops, one_hop, 0)


def shards(sizes, rows, path, norm_gain, gate_weight, up_weight, down_weight):
    ep, tp, sub, cap, per_chunk = sizes
    local_rows, quarter = rows.shape
    hops = path.shape[0]
    hid, width = gate_weight.shape[1:]
    half = quarter * tp
    experts = ep * tp
    chunks = ep // per_chunk
    dma = pltpu.SemaphoreType.DMA
    vmem, any_space = pl.BlockSpec(memory_space=pltpu.VMEM), pl.BlockSpec(memory_space=pl.ANY)
    return pl.pallas_call(
        functools.partial(chain_kernel, sizes),
        out_shape=jax.ShapeDtypeStruct(rows.shape, rows.dtype),
        in_specs=[vmem, vmem, vmem, any_space, any_space, any_space],
        out_specs=vmem,
        scratch_shapes=[
            pltpu.VMEM((1, hid, width), BF16),
            pltpu.VMEM((1, hid, width), BF16),
            pltpu.VMEM((1, hid, width), BF16),
            pltpu.VMEM((hops, experts * cap, local_rows), BF16),
            pltpu.VMEM((experts, cap, quarter), BF16),
            pltpu.VMEM((sub * tp, ep * cap, quarter), BF16),
            pltpu.VMEM((ep * cap, width), BF16),
            pltpu.VMEM((ep * cap, hid), BF16),
            pltpu.VMEM((sub - 1, ep * cap, half), BF16),
            pltpu.VMEM((sub - 1, ep * cap, half), BF16),
            pltpu.VMEM((ep * cap, half), F32),
            pltpu.VMEM((tp, ep * cap, quarter), BF16),
            pltpu.VMEM((experts, cap, quarter), BF16),
            dma((3,)),
            dma((ep, tp)),
            dma((ep, tp)),
            dma((ep, sub - 1)),
            dma((ep, sub - 1)),
            dma((chunks, sub - 1)),
            dma((chunks, sub - 1)),
            dma((ep, tp)),
            dma((ep, tp)),
        ],
        compiler_params=pltpu.CompilerParams(
            collective_id=0, has_side_effects=True, vmem_limit_bytes=48 * 1024 * 1024
        ),
        cost_estimate=pl.CostEstimate(
            flops=2 * hops * ep * cap * hid * width * 3,
            bytes_accessed=3 * hid * width * 2,
            transcendentals=hops * ep * cap * hid,
        ),
    )(rows, path[:, :, 0], norm_gain, gate_weight, up_weight, down_weight)


def solution(mesh):
    ep, tp, sub = mesh.shape["ep"], mesh.shape["tp"], mesh.shape["sub"]

    def run(rows, path, norm_gain, gate_weight, up_weight, down_weight):
        cap = max(16, 2 * rows.shape[0] // (ep * tp))
        sizes = (ep, tp, sub, cap, ep // 2)
        return shards(sizes, rows, path, norm_gain, gate_weight, up_weight, down_weight)

    in_specs = (
        P(("groups", "ep"), ("sub", "tp")),
        P(None, ("groups", "ep"), None),
        P(("ep", "tp"), None),
        P(("ep", "tp"), "sub", None),
        P(("ep", "tp"), "sub", None),
        P(("ep", "tp"), "sub", None),
    )
    out_specs = P(("groups", "ep"), ("sub", "tp"))
    return jax.shard_map(run, mesh=mesh, in_specs=in_specs, out_specs=out_specs, check_vma=False)
```

```python
import functools

import jax
import jax.numpy as jnp
from jax import lax
from jax.experimental import pallas as pl
from jax.experimental.pallas import tpu as pltpu
from jax.sharding import PartitionSpec as P

EPS = 1e-06
MESH = pl.DeviceIdType.MESH
F32 = jnp.float32
BF16 = jnp.bfloat16


def partner(index, distance, count):
    out, bit = 0, 1
    while bit < count:
        own = (index // bit) % 2
        out = out + bit * ((1 - own) if (distance // bit) % 2 else own)
        bit *= 2
    return out


def chain_kernel(
    sizes,
    rows_hbm,
    path_hbm,
    gain_hbm,
    gate_hbm,
    up_hbm,
    down_hbm,
    state_ref,
    path_ref,
    gain_ref,
    gate_ref,
    up_ref,
    down_ref,
    placing_ref,
    taking_ref,
    packed_ref,
    arrived_ref,
    normed_ref,
    hidden_ref,
    part_out_ref,
    part_in_ref,
    own_ref,
    summed_ref,
    returned_ref,
    load_sem,
    disp_send,
    disp_recv,
    fwd_send,
    fwd_recv,
    part_send,
    part_recv,
    ret_send,
    ret_recv,
):
    ep, tp, sub, cap = sizes
    z, s, t = lax.axis_index("ep"), lax.axis_index("sub"), lax.axis_index("tp")
    hops = path_ref.shape[0]
    local_rows, quarter = state_ref.shape
    half = quarter * tp
    experts = ep * tp
    chunks = ep // 2
    pairs = [(chunks + i, i) for i in range(chunks)]
    order = [k for pair in pairs for k in pair]
    chunk_rows = 2 * cap
    here = s * tp + t

    loads = [
        pltpu.make_async_copy(src, dst, load_sem.at[i])
        for i, (src, dst) in enumerate(
            (
                (rows_hbm, state_ref),
                (path_hbm, path_ref),
                (gate_hbm, gate_ref),
                (up_hbm, up_ref),
                (down_hbm, down_ref),
                (gain_hbm, gain_ref),
            )
        )
    ]
    for load in loads:
        load.start()

    barrier = pltpu.get_barrier_semaphore()
    peers = 0
    for k in range(ep):
        for c in range(tp):
            if k or c:
                pl.semaphore_signal(
                    barrier, inc=1,
                    device_id={"ep": partner(z, k, ep), "tp": (t + c) % tp},
                    device_id_type=MESH,
                )
                peers += 1
    for j in range(1, sub):
        pl.semaphore_signal(
            barrier, inc=1, device_id={"sub": (s + j) % sub}, device_id_type=MESH
        )
        peers += 1

    def rows_of(k):
        return pl.ds(order.index(k) * cap, cap)

    def rows_in(chunk):
        return pl.ds(chunk * chunk_rows, chunk_rows)

    def dispatch_copy(k, c):
        to_z, to_t = partner(z, k, ep), (t + c) % tp
        return pltpu.make_async_remote_copy(
            src_ref=packed_ref.at[to_z * tp + to_t],
            dst_ref=arrived_ref.at[here, rows_of(k)],
            send_sem=disp_send.at[k, c],
            recv_sem=disp_recv.at[k, c],
            device_id={"ep": to_z, "tp": to_t},
            device_id_type=MESH,
        )

    def forward_copy(k, j):
        block = arrived_ref.at[pl.ds(s * tp, tp), rows_of(k)]
        return pltpu.make_async_remote_copy(
            src_ref=block,
            dst_ref=block,
            send_sem=fwd_send.at[k, j - 1],
            recv_sem=fwd_recv.at[k, j - 1],
            device_id={"sub": (s + j) % sub},
            device_id_type=MESH,
        )

    def part_copy(k, j):
        return pltpu.make_async_remote_copy(
            src_ref=part_out_ref.at[j - 1, rows_of(k)],
            dst_ref=part_in_ref.at[j - 1, rows_of(k)],
            send_sem=part_send.at[k, j - 1],
            recv_sem=part_recv.at[k, j - 1],
            device_id={"sub": (s + j) % sub},
            device_id_type=MESH,
        )

    def return_copy(k, c):
        to_z, to_t = partner(z, k, ep), (t + c) % tp
        return pltpu.make_async_remote_copy(
            src_ref=summed_ref.at[to_t, rows_of(k)],
            dst_ref=returned_ref.at[z * tp + t],
            send_sem=ret_send.at[k, c],
            recv_sem=ret_recv.at[k, c],
            device_id={"ep": to_z, "tp": to_t},
            device_id_type=MESH,
        )

    remote = [(k, c) for k in range(ep) for c in range(tp) if k or c]
    own_first = [0] + list(range(chunks, ep)) + list(range(1, chunks))

    def make_placing(hop):
        named = path_ref[pl.ds(hop, 1), :]
        lines = -(-experts // 8) * 8
        onehot = (
            lax.broadcasted_iota(jnp.int32, (lines, local_rows), 0) == named
        ).astype(F32)
        earlier = (
            lax.broadcasted_iota(jnp.int32, (local_rows, local_rows), 0)
            < lax.broadcasted_iota(jnp.int32, (local_rows, local_rows), 1)
        ).astype(F32)
        before = jnp.dot(
            onehot.astype(BF16), earlier.astype(BF16), preferred_element_type=F32
        )
        rank = jnp.sum(before * onehot, axis=0, keepdims=True)
        target = named.astype(F32) * float(cap) + rank
        slots = lax.broadcasted_iota(jnp.int32, (experts * cap, local_rows), 0)
        placing_ref[hop] = jnp.where(slots.astype(F32) == target, 1.0, 0.0).astype(BF16)

    def dispatch(hop):
        for k in own_first:
            first = partner(z, k, ep) * tp
            lines = pl.ds(pl.multiple_of(first * cap, 16), tp * cap)
            packed = jnp.dot(
                placing_ref[hop, lines, :], state_ref[...], preferred_element_type=F32
            ).astype(BF16)
            for i in range(tp):
                packed_ref[first + i] = packed[i * cap : (i + 1) * cap]
            for c in range(tp):
                if k or c:
                    dispatch_copy(k, c).start()
                else:
                    arrived_ref[here, rows_of(0), :] = packed_ref[z * tp + t]

    def forward(k):
        for c in range(tp):
            if k or c:
                dispatch_copy(k, c).wait_recv()
        for j in range(1, sub):
            forward_copy(k, j).start()

    def normalise(k):
        for j in range(1, sub):
            forward_copy(k, j).wait_recv()
        total = jnp.zeros((cap, 1), F32)
        for q in range(sub * tp):
            value = arrived_ref[q, rows_of(k), :].astype(F32)
            total = total + jnp.sum(value * value, axis=-1, keepdims=True)
        scale = lax.rsqrt(total / float(quarter * sub * tp) + EPS)
        for q in range(sub * tp):
            value = arrived_ref[q, rows_of(k), :].astype(F32)
            columns = pl.ds(q * quarter, quarter)
            normed_ref[rows_of(k), columns] = (
                value * scale * gain_ref[:, columns]
            ).astype(BF16)

    def expand(chunk):
        for k in pairs[chunk]:
            normalise(k)
        normed = normed_ref[rows_in(chunk), :]
        dims = (((1,), (1,)), ((), ()))
        gate = lax.dot_general(normed, gate_ref[0], dims, preferred_element_type=F32)
        upward = lax.dot_general(normed, up_ref[0], dims, preferred_element_type=F32)
        hidden_ref[rows_in(chunk), :] = (
            gate / (1.0 + jnp.exp(-gate)) * upward
        ).astype(BF16)

    tile = min(512, half)

    def contract(chunk, j, out):
        base = ((s + j) % sub) * half

        def step(i, carry):
            inside = pl.ds(pl.multiple_of(i * tile, tile), tile)
            columns = pl.ds(pl.multiple_of(base + i * tile, tile), tile)
            out[rows_in(chunk), inside] = jnp.dot(
                hidden_ref[rows_in(chunk), :],
                down_ref[0, :, columns],
                preferred_element_type=F32,
            ).astype(out.dtype)
            return carry

        lax.fori_loop(0, half // tile, step, 0)

    def project(chunk):
        for j in range(1, sub):
            contract(chunk, j, part_out_ref.at[j - 1])
            for k in pairs[chunk]:
                part_copy(k, j).start()
        contract(chunk, 0, own_ref)

    def give_back(chunk):
        for k in pairs[chunk]:
            for j in range(1, sub):
                part_copy(k, j).wait_recv()
            for i in range(tp):
                columns = pl.ds(i * quarter, quarter)
                value = own_ref[rows_of(k), columns]
                for j in range(1, sub):
                    value = value + part_in_ref[j - 1, rows_of(k), columns].astype(F32)
                summed_ref[i, rows_of(k), :] = value.astype(BF16)
            for c in range(tp):
                if k or c:
                    return_copy(k, c).start()
                else:
                    returned_ref[z * tp + t] = summed_ref[t, rows_of(k), :]

    for load in loads[:2]:
        load.wait()
    make_placing(0)
    pl.semaphore_wait(barrier, peers)
    dispatch(0)
    for hop in range(1, hops):
        make_placing(hop)
    for hop in range(hops):
        taking_ref[hop] = placing_ref[hop].T
    for load in loads[2:]:
        load.wait()

    def one_hop(hop, carry):
        for k in pairs[0][::-1]:
            forward(k)
        expand(0)
        for chunk in range(1, chunks):
            for k in pairs[chunk][::-1]:
                forward(k)
            project(chunk - 1)
            expand(chunk)
        project(chunks - 1)
        for k in range(ep):
            for j in range(1, sub):
                forward_copy(k, j).wait_send()
        for chunk in range(chunks):
            give_back(chunk)
        for k, c in remote:
            dispatch_copy(k, c).wait_send()
        for k, c in remote:
            return_copy(k, c).wait_recv()
        update = jnp.dot(
            taking_ref[hop],
            returned_ref[...].reshape(experts * cap, quarter),
            preferred_element_type=F32,
        )
        state_ref[...] = (state_ref[...].astype(F32) + update).astype(BF16)

        @pl.when(hop < hops - 1)
        def _():
            dispatch(hop + 1)

        for k in range(ep):
            for j in range(1, sub):
                part_copy(k, j).wait_send()
        for k, c in remote:
            return_copy(k, c).wait_send()
        return carry

    lax.fori_loop(0, hops, one_hop, 0)


def shards(sizes, rows, path, norm_gain, gate_weight, up_weight, down_weight):
    ep, tp, sub, cap = sizes
    local_rows, quarter = rows.shape
    hops = path.shape[0]
    hid, width = gate_weight.shape[1:]
    half = quarter * tp
    experts = ep * tp
    dma = pltpu.SemaphoreType.DMA
    vmem, any_space = pl.BlockSpec(memory_space=pltpu.VMEM), pl.BlockSpec(memory_space=pl.ANY)
    return pl.pallas_call(
        functools.partial(chain_kernel, sizes),
        out_shape=jax.ShapeDtypeStruct(rows.shape, rows.dtype),
        in_specs=[any_space] * 6,
        out_specs=vmem,
        scratch_shapes=[
            pltpu.VMEM((hops, local_rows), jnp.int32),
            pltpu.VMEM((1, width), F32),
            pltpu.VMEM((1, hid, width), BF16),
            pltpu.VMEM((1, hid, width), BF16),
            pltpu.VMEM((1, hid, width), BF16),
            pltpu.VMEM((hops, experts * cap, local_rows), BF16),
            pltpu.VMEM((hops, local_rows, experts * cap), BF16),
            pltpu.VMEM((experts, cap, quarter), BF16),
            pltpu.VMEM((sub * tp, ep * cap, quarter), BF16),
            pltpu.VMEM((ep * cap, width), BF16),
            pltpu.VMEM((ep * cap, hid), BF16),
            pltpu.VMEM((sub - 1, ep * cap, half), BF16),
            pltpu.VMEM((sub - 1, ep * cap, half), BF16),
            pltpu.VMEM((ep * cap, half), F32),
            pltpu.VMEM((tp, ep * cap, quarter), BF16),
            pltpu.VMEM((experts, cap, quarter), BF16),
            dma((6,)),
            dma((ep, tp)),
            dma((ep, tp)),
            dma((ep, sub - 1)),
            dma((ep, sub - 1)),
            dma((ep, sub - 1)),
            dma((ep, sub - 1)),
            dma((ep, tp)),
            dma((ep, tp)),
        ],
        compiler_params=pltpu.CompilerParams(
            collective_id=0, has_side_effects=True, vmem_limit_bytes=56 * 1024 * 1024
        ),
        cost_estimate=pl.CostEstimate(
            flops=2 * hops * ep * cap * hid * width * 3,
            bytes_accessed=3 * hid * width * 2,
            transcendentals=hops * ep * cap * hid,
        ),
    )(rows, path[:, :, 0], norm_gain, gate_weight, up_weight, down_weight)


def solution(mesh):
    ep, tp, sub = mesh.shape["ep"], mesh.shape["tp"], mesh.shape["sub"]

    def run(rows, path, norm_gain, gate_weight, up_weight, down_weight):
        cap = max(16, 2 * rows.shape[0] // (ep * tp))
        sizes = (ep, tp, sub, cap)
        return shards(sizes, rows, path, norm_gain, gate_weight, up_weight, down_weight)

    in_specs = (
        P(("groups", "ep"), ("sub", "tp")),
        P(None, ("groups", "ep"), None),
        P(("ep", "tp"), None),
        P(("ep", "tp"), "sub", None),
        P(("ep", "tp"), "sub", None),
        P(("ep", "tp"), "sub", None),
    )
    out_specs = P(("groups", "ep"), ("sub", "tp"))
    return jax.shard_map(run, mesh=mesh, in_specs=in_specs, out_specs=out_specs, check_vma=False)
```

```python
import functools

import jax
import jax.numpy as jnp
from jax import lax
from jax.experimental import pallas as pl
from jax.experimental.pallas import tpu as pltpu
from jax.sharding import PartitionSpec as P

EPS = 1e-06
MESH = pl.DeviceIdType.MESH
F32 = jnp.float32
BF16 = jnp.bfloat16


def partner(index, distance, count):
    out, bit = 0, 1
    while bit < count:
        own = (index // bit) % 2
        out = out + bit * ((1 - own) if (distance // bit) % 2 else own)
        bit *= 2
    return out


def chain_kernel(
    sizes,
    rows_hbm,
    path_hbm,
    gain_hbm,
    gate_hbm,
    up_hbm,
    down_hbm,
    state_ref,
    path_ref,
    gain_ref,
    gate_ref,
    up_ref,
    down_ref,
    turned_ref,
    placing_ref,
    taking_ref,
    packed_ref,
    arrived_ref,
    normed_ref,
    hidden_ref,
    part_out_ref,
    part_in_ref,
    own_ref,
    summed_ref,
    returned_ref,
    load_sem,
    disp_send,
    disp_recv,
    fwd_send,
    fwd_recv,
    part_send,
    part_recv,
    ret_send,
    ret_recv,
):
    ep, tp, sub, cap = sizes
    z, s, t = lax.axis_index("ep"), lax.axis_index("sub"), lax.axis_index("tp")
    hops = path_ref.shape[0]
    local_rows, quarter = state_ref.shape
    half = quarter * tp
    experts = ep * tp
    chunks = ep // 2
    pairs = [(chunks + i, i) for i in range(chunks)]
    order = [k for pair in pairs for k in pair]
    chunk_rows = 2 * cap
    here = s * tp + t

    loads = [
        pltpu.make_async_copy(src, dst, load_sem.at[i])
        for i, (src, dst) in enumerate(
            (
                (rows_hbm, state_ref),
                (path_hbm, path_ref),
                (gate_hbm, gate_ref),
                (up_hbm, up_ref),
                (down_hbm, down_ref),
                (gain_hbm, gain_ref),
            )
        )
    ]
    for load in loads:
        load.start()

    barrier = pltpu.get_barrier_semaphore()
    peers = 0
    for k in range(ep):
        for c in range(tp):
            if k or c:
                pl.semaphore_signal(
                    barrier, inc=1,
                    device_id={"ep": partner(z, k, ep), "tp": (t + c) % tp},
                    device_id_type=MESH,
                )
                peers += 1
    for j in range(1, sub):
        pl.semaphore_signal(
            barrier, inc=1, device_id={"sub": (s + j) % sub}, device_id_type=MESH
        )
        peers += 1

    def rows_of(k):
        return pl.ds(order.index(k) * cap, cap)

    def rows_in(chunk):
        return pl.ds(chunk * chunk_rows, chunk_rows)

    def dispatch_copy(k, c):
        to_z, to_t = partner(z, k, ep), (t + c) % tp
        return pltpu.make_async_remote_copy(
            src_ref=packed_ref.at[to_z * tp + to_t],
            dst_ref=arrived_ref.at[here, rows_of(k)],
            send_sem=disp_send.at[k, c],
            recv_sem=disp_recv.at[k, c],
            device_id={"ep": to_z, "tp": to_t},
            device_id_type=MESH,
        )

    def forward_copy(k, j):
        block = arrived_ref.at[pl.ds(s * tp, tp), rows_of(k)]
        return pltpu.make_async_remote_copy(
            src_ref=block,
            dst_ref=block,
            send_sem=fwd_send.at[k, j - 1],
            recv_sem=fwd_recv.at[k, j - 1],
            device_id={"sub": (s + j) % sub},
            device_id_type=MESH,
        )

    def part_copy(k, j):
        return pltpu.make_async_remote_copy(
            src_ref=part_out_ref.at[j - 1, rows_of(k)],
            dst_ref=part_in_ref.at[j - 1, rows_of(k)],
            send_sem=part_send.at[k, j - 1],
            recv_sem=part_recv.at[k, j - 1],
            device_id={"sub": (s + j) % sub},
            device_id_type=MESH,
        )

    def return_copy(k, c):
        to_z, to_t = partner(z, k, ep), (t + c) % tp
        return pltpu.make_async_remote_copy(
            src_ref=summed_ref.at[to_t, rows_of(k)],
            dst_ref=returned_ref.at[z * tp + t],
            send_sem=ret_send.at[k, c],
            recv_sem=ret_recv.at[k, c],
            device_id={"ep": to_z, "tp": to_t},
            device_id_type=MESH,
        )

    remote = [(k, c) for k in range(ep) for c in range(tp) if k or c]
    own_first = [0] + list(range(chunks, ep)) + list(range(1, chunks))

    def make_placing(hop):
        named = path_ref[pl.ds(hop, 1), :]
        lines = -(-experts // 8) * 8
        onehot = (
            lax.broadcasted_iota(jnp.int32, (lines, local_rows), 0) == named
        ).astype(F32)
        earlier = (
            lax.broadcasted_iota(jnp.int32, (local_rows, local_rows), 0)
            < lax.broadcasted_iota(jnp.int32, (local_rows, local_rows), 1)
        ).astype(F32)
        before = jnp.dot(
            onehot.astype(BF16), earlier.astype(BF16), preferred_element_type=F32
        )
        rank = jnp.sum(before * onehot, axis=0, keepdims=True)
        target = named.astype(F32) * float(cap) + rank
        slots = lax.broadcasted_iota(jnp.int32, (experts * cap, local_rows), 0)
        placing_ref[hop] = jnp.where(slots.astype(F32) == target, 1.0, 0.0).astype(BF16)

    def dispatch(hop):
        for k in own_first:
            first = partner(z, k, ep) * tp
            lines = pl.ds(pl.multiple_of(first * cap, 16), tp * cap)
            packed = jnp.dot(
                placing_ref[hop, lines, :], state_ref[...], preferred_element_type=F32
            ).astype(BF16)
            for i in range(tp):
                packed_ref[first + i] = packed[i * cap : (i + 1) * cap]
            for c in range(tp):
                if k or c:
                    dispatch_copy(k, c).start()
                else:
                    arrived_ref[here, rows_of(0), :] = packed_ref[z * tp + t]

    def forward(k):
        for c in range(tp):
            if k or c:
                dispatch_copy(k, c).wait_recv()
        for j in range(1, sub):
            forward_copy(k, j).start()

    def normalise(k):
        for j in range(1, sub):
            forward_copy(k, j).wait_recv()
        total = jnp.zeros((cap, 1), F32)
        for q in range(sub * tp):
            value = arrived_ref[q, rows_of(k), :].astype(F32)
            total = total + jnp.sum(value * value, axis=-1, keepdims=True)
        scale = lax.rsqrt(total / float(quarter * sub * tp) + EPS)
        for q in range(sub * tp):
            value = arrived_ref[q, rows_of(k), :].astype(F32)
            columns = pl.ds(q * quarter, quarter)
            normed_ref[rows_of(k), columns] = (
                value * scale * gain_ref[:, columns]
            ).astype(BF16)

    def expand(chunk):
        for k in pairs[chunk]:
            normalise(k)
        normed = normed_ref[rows_in(chunk), :]
        dims = (((1,), (1,)), ((), ()))
        gate = lax.dot_general(gate_ref[0], normed, dims, preferred_element_type=F32)
        upward = lax.dot_general(up_ref[0], normed, dims, preferred_element_type=F32)
        hidden_ref[chunk] = (gate / (1.0 + jnp.exp(-gate)) * upward).astype(BF16)

    tile = min(512, half)

    def contract(chunk, j, out):
        base = ((s + j) % sub) * half

        def step(i, carry):
            inside = pl.ds(pl.multiple_of(i * tile, tile), tile)
            columns = pl.ds(pl.multiple_of(base + i * tile, tile), tile)
            product = jnp.dot(
                turned_ref[columns, :], hidden_ref[chunk], preferred_element_type=F32
            )
            out[rows_in(chunk), inside] = product.T.astype(out.dtype)
            return carry

        lax.fori_loop(0, half // tile, step, 0)

    def project(chunk):
        for j in range(1, sub):
            contract(chunk, j, part_out_ref.at[j - 1])
            for k in pairs[chunk]:
                part_copy(k, j).start()
        contract(chunk, 0, own_ref)

    def give_back(chunk):
        for k in pairs[chunk]:
            for j in range(1, sub):
                part_copy(k, j).wait_recv()
            for i in range(tp):
                columns = pl.ds(i * quarter, quarter)
                value = own_ref[rows_of(k), columns]
                for j in range(1, sub):
                    value = value + part_in_ref[j - 1, rows_of(k), columns].astype(F32)
                summed_ref[i, rows_of(k), :] = value.astype(BF16)
            for c in range(tp):
                if k or c:
                    return_copy(k, c).start()
                else:
                    returned_ref[z * tp + t] = summed_ref[t, rows_of(k), :]

    for load in loads[:2]:
        load.wait()
    make_placing(0)
    pl.semaphore_wait(barrier, peers)
    dispatch(0)
    for hop in range(1, hops):
        make_placing(hop)
    for hop in range(hops):
        taking_ref[hop] = placing_ref[hop].T
    for load in loads[2:]:
        load.wait()

    def turn(i, carry):
        columns = pl.ds(pl.multiple_of(i * tile, tile), tile)
        turned_ref[columns, :] = down_ref[0, :, columns].T
        return carry

    lax.fori_loop(0, turned_ref.shape[0] // tile, turn, 0)

    def one_hop(hop, carry):
        for k in pairs[0][::-1]:
            forward(k)
        expand(0)
        for chunk in range(1, chunks):
            for k in pairs[chunk][::-1]:
                forward(k)
            project(chunk - 1)
            expand(chunk)
        project(chunks - 1)
        for k in range(ep):
            for j in range(1, sub):
                forward_copy(k, j).wait_send()
        for chunk in range(chunks):
            give_back(chunk)
        for k, c in remote:
            dispatch_copy(k, c).wait_send()
        for k, c in remote:
            return_copy(k, c).wait_recv()
        update = jnp.dot(
            taking_ref[hop],
            returned_ref[...].reshape(experts * cap, quarter),
            preferred_element_type=F32,
        )
        state_ref[...] = (state_ref[...].astype(F32) + update).astype(BF16)

        @pl.when(hop < hops - 1)
        def _():
            dispatch(hop + 1)

        for k in range(ep):
            for j in range(1, sub):
                part_copy(k, j).wait_send()
        for k, c in remote:
            return_copy(k, c).wait_send()
        return carry

    lax.fori_loop(0, hops, one_hop, 0)


def shards(sizes, rows, path, norm_gain, gate_weight, up_weight, down_weight):
    ep, tp, sub, cap = sizes
    local_rows, quarter = rows.shape
    hops = path.shape[0]
    hid, width = gate_weight.shape[1:]
    half = quarter * tp
    experts = ep * tp
    dma = pltpu.SemaphoreType.DMA
    vmem, any_space = pl.BlockSpec(memory_space=pltpu.VMEM), pl.BlockSpec(memory_space=pl.ANY)
    return pl.pallas_call(
        functools.partial(chain_kernel, sizes),
        out_shape=jax.ShapeDtypeStruct(rows.shape, rows.dtype),
        in_specs=[any_space] * 6,
        out_specs=vmem,
        scratch_shapes=[
            pltpu.VMEM((hops, local_rows), jnp.int32),
            pltpu.VMEM((1, width), F32),
            pltpu.VMEM((1, hid, width), BF16),
            pltpu.VMEM((1, hid, width), BF16),
            pltpu.VMEM((1, hid, width), BF16),
            pltpu.VMEM((width, hid), BF16),
            pltpu.VMEM((hops, experts * cap, local_rows), BF16),
            pltpu.VMEM((hops, local_rows, experts * cap), BF16),
            pltpu.VMEM((experts, cap, quarter), BF16),
            pltpu.VMEM((sub * tp, ep * cap, quarter), BF16),
            pltpu.VMEM((ep * cap, width), BF16),
            pltpu.VMEM((ep // 2, hid, 2 * cap), BF16),
            pltpu.VMEM((sub - 1, ep * cap, half), BF16),
            pltpu.VMEM((sub - 1, ep * cap, half), BF16),
            pltpu.VMEM((ep * cap, half), F32),
            pltpu.VMEM((tp, ep * cap, quarter), BF16),
            pltpu.VMEM((experts, cap, quarter), BF16),
            dma((6,)),
            dma((ep, tp)),
            dma((ep, tp)),
            dma((ep, sub - 1)),
            dma((ep, sub - 1)),
            dma((ep, sub - 1)),
            dma((ep, sub - 1)),
            dma((ep, tp)),
            dma((ep, tp)),
        ],
        compiler_params=pltpu.CompilerParams(
            collective_id=0, has_side_effects=True, vmem_limit_bytes=56 * 1024 * 1024
        ),
        cost_estimate=pl.CostEstimate(
            flops=2 * hops * ep * cap * hid * width * 3,
            bytes_accessed=3 * hid * width * 2,
            transcendentals=hops * ep * cap * hid,
        ),
    )(rows, path[:, :, 0], norm_gain, gate_weight, up_weight, down_weight)


def solution(mesh):
    ep, tp, sub = mesh.shape["ep"], mesh.shape["tp"], mesh.shape["sub"]

    def run(rows, path, norm_gain, gate_weight, up_weight, down_weight):
        cap = max(16, 2 * rows.shape[0] // (ep * tp))
        sizes = (ep, tp, sub, cap)
        return shards(sizes, rows, path, norm_gain, gate_weight, up_weight, down_weight)

    in_specs = (
        P(("groups", "ep"), ("sub", "tp")),
        P(None, ("groups", "ep"), None),
        P(("ep", "tp"), None),
        P(("ep", "tp"), "sub", None),
        P(("ep", "tp"), "sub", None),
        P(("ep", "tp"), "sub", None),
    )
    out_specs = P(("groups", "ep"), ("sub", "tp"))
    return jax.shard_map(run, mesh=mesh, in_specs=in_specs, out_specs=out_specs, check_vma=False)
```

```python
import functools

import jax
import jax.numpy as jnp
from jax import lax
from jax.experimental import pallas as pl
from jax.experimental.pallas import tpu as pltpu
from jax.sharding import PartitionSpec as P

EPS = 1e-06
MESH = pl.DeviceIdType.MESH
F32 = jnp.float32
BF16 = jnp.bfloat16


def partner(index, distance, count):
    out, bit = 0, 1
    while bit < count:
        own = (index // bit) % 2
        out = out + bit * ((1 - own) if (distance // bit) % 2 else own)
        bit *= 2
    return out


def chain_kernel(
    sizes,
    rows_hbm,
    path_hbm,
    gain_hbm,
    gate_hbm,
    up_hbm,
    down_hbm,
    state_ref,
    path_ref,
    gain_ref,
    gate_ref,
    up_ref,
    down_ref,
    turned_ref,
    placing_ref,
    taking_ref,
    packed_ref,
    arrived_ref,
    normed_ref,
    hidden_ref,
    part_out_ref,
    part_in_ref,
    own_ref,
    summed_ref,
    returned_ref,
    load_sem,
    disp_send,
    disp_recv,
    fwd_send,
    fwd_recv,
    part_send,
    part_recv,
    ret_send,
    ret_recv,
):
    ep, tp, sub, cap = sizes
    z, s, t = lax.axis_index("ep"), lax.axis_index("sub"), lax.axis_index("tp")
    hops = path_ref.shape[0]
    local_rows, quarter = state_ref.shape
    half = quarter * tp
    experts = ep * tp
    chunks = ep // 2
    pairs = [(chunks + i, i) for i in range(chunks)]
    order = [k for pair in pairs for k in pair]
    chunk_rows = 2 * cap
    here = s * tp + t

    loads = [
        pltpu.make_async_copy(src, dst, load_sem.at[i])
        for i, (src, dst) in enumerate(
            (
                (rows_hbm, state_ref),
                (path_hbm, path_ref),
                (gate_hbm, gate_ref),
                (up_hbm, up_ref),
                (down_hbm, down_ref),
                (gain_hbm, gain_ref),
            )
        )
    ]
    for load in loads:
        load.start()

    barrier = pltpu.get_barrier_semaphore()
    peers = 0
    for k in range(ep):
        for c in range(tp):
            if k or c:
                pl.semaphore_signal(
                    barrier, inc=1,
                    device_id={"ep": partner(z, k, ep), "tp": (t + c) % tp},
                    device_id_type=MESH,
                )
                peers += 1
    for j in range(1, sub):
        pl.semaphore_signal(
            barrier, inc=1, device_id={"sub": (s + j) % sub}, device_id_type=MESH
        )
        peers += 1

    def rows_of(k):
        return pl.ds(order.index(k) * cap, cap)

    def rows_in(chunk):
        return pl.ds(chunk * chunk_rows, chunk_rows)

    def dispatch_copy(k, c):
        to_z, to_t = partner(z, k, ep), (t + c) % tp
        return pltpu.make_async_remote_copy(
            src_ref=packed_ref.at[to_z * tp + to_t],
            dst_ref=arrived_ref.at[here, rows_of(k)],
            send_sem=disp_send.at[k, c],
            recv_sem=disp_recv.at[k, c],
            device_id={"ep": to_z, "tp": to_t},
            device_id_type=MESH,
        )

    def forward_copy(k, j):
        block = arrived_ref.at[pl.ds(s * tp, tp), rows_of(k)]
        return pltpu.make_async_remote_copy(
            src_ref=block,
            dst_ref=block,
            send_sem=fwd_send.at[k, j - 1],
            recv_sem=fwd_recv.at[k, j - 1],
            device_id={"sub": (s + j) % sub},
            device_id_type=MESH,
        )

    def part_copy(k, j):
        return pltpu.make_async_remote_copy(
            src_ref=part_out_ref.at[j - 1, rows_of(k)],
            dst_ref=part_in_ref.at[j - 1, rows_of(k)],
            send_sem=part_send.at[k, j - 1],
            recv_sem=part_recv.at[k, j - 1],
            device_id={"sub": (s + j) % sub},
            device_id_type=MESH,
        )

    def return_copy(k, c):
        to_z, to_t = partner(z, k, ep), (t + c) % tp
        return pltpu.make_async_remote_copy(
            src_ref=summed_ref.at[to_t, rows_of(k)],
            dst_ref=returned_ref.at[z * tp + t],
            send_sem=ret_send.at[k, c],
            recv_sem=ret_recv.at[k, c],
            device_id={"ep": to_z, "tp": to_t},
            device_id_type=MESH,
        )

    remote = [(k, c) for k in range(ep) for c in range(tp) if k or c]
    own_first = [0] + list(range(chunks, ep)) + list(range(1, chunks))

    def make_placing(hop):
        named = path_ref[pl.ds(hop, 1), :]
        lines = -(-experts // 8) * 8
        onehot = (
            lax.broadcasted_iota(jnp.int32, (lines, local_rows), 0) == named
        ).astype(F32)
        earlier = (
            lax.broadcasted_iota(jnp.int32, (local_rows, local_rows), 0)
            < lax.broadcasted_iota(jnp.int32, (local_rows, local_rows), 1)
        ).astype(F32)
        before = jnp.dot(
            onehot.astype(BF16), earlier.astype(BF16), preferred_element_type=F32
        )
        rank = jnp.sum(before * onehot, axis=0, keepdims=True)
        target = named.astype(F32) * float(cap) + rank
        slots = lax.broadcasted_iota(jnp.int32, (experts * cap, local_rows), 0)
        placing_ref[hop] = jnp.where(slots.astype(F32) == target, 1.0, 0.0).astype(BF16)

    def dispatch(hop):
        for k in own_first:
            first = partner(z, k, ep) * tp
            lines = pl.ds(pl.multiple_of(first * cap, 16), tp * cap)
            packed = jnp.dot(
                placing_ref[hop, lines, :], state_ref[...], preferred_element_type=F32
            ).astype(BF16)
            for i in range(tp):
                packed_ref[first + i] = packed[i * cap : (i + 1) * cap]
        arrived_ref[here, rows_of(0), :] = packed_ref[z * tp + t]
        send(0)

    def send(k):
        for c in range(tp):
            if k or c:
                dispatch_copy(k, c).start()

    def arrive(k):
        for c in range(tp):
            if k or c:
                dispatch_copy(k, c).wait_recv()

    def forward(k):
        for j in range(1, sub):
            forward_copy(k, j).start()

    def either(first, second):
        @pl.when(t % 2 == 0)
        def _():
            first()
            second()

        @pl.when(t % 2 == 1)
        def _():
            second()
            first()

    def normalise(k):
        for j in range(1, sub):
            forward_copy(k, j).wait_recv()
        total = jnp.zeros((cap, 1), F32)
        for q in range(sub * tp):
            value = arrived_ref[q, rows_of(k), :].astype(F32)
            total = total + jnp.sum(value * value, axis=-1, keepdims=True)
        scale = lax.rsqrt(total / float(quarter * sub * tp) + EPS)
        for q in range(sub * tp):
            value = arrived_ref[q, rows_of(k), :].astype(F32)
            columns = pl.ds(q * quarter, quarter)
            normed_ref[rows_of(k), columns] = (
                value * scale * gain_ref[:, columns]
            ).astype(BF16)

    def expand(chunk):
        for k in pairs[chunk]:
            normalise(k)
        normed = normed_ref[rows_in(chunk), :]
        dims = (((1,), (1,)), ((), ()))
        gate = lax.dot_general(gate_ref[0], normed, dims, preferred_element_type=F32)
        upward = lax.dot_general(up_ref[0], normed, dims, preferred_element_type=F32)
        hidden_ref[chunk] = (gate / (1.0 + jnp.exp(-gate)) * upward).astype(BF16)

    tile = min(512, half)

    def contract(chunk, j, out):
        base = ((s + j) % sub) * half

        def step(i, carry):
            inside = pl.ds(pl.multiple_of(i * tile, tile), tile)
            columns = pl.ds(pl.multiple_of(base + i * tile, tile), tile)
            product = jnp.dot(
                turned_ref[columns, :], hidden_ref[chunk], preferred_element_type=F32
            )
            out[rows_in(chunk), inside] = product.T.astype(out.dtype)
            return carry

        lax.fori_loop(0, half // tile, step, 0)

    def project(chunk):
        for j in range(1, sub):
            contract(chunk, j, part_out_ref.at[j - 1])
        contract(chunk, 0, own_ref)

    def exchange(chunk):
        for k in pairs[chunk]:
            for j in range(1, sub):
                part_copy(k, j).start()

    def sum_up(chunk):
        for k in pairs[chunk]:
            for j in range(1, sub):
                part_copy(k, j).wait_recv()
            for i in range(tp):
                columns = pl.ds(i * quarter, quarter)
                value = own_ref[rows_of(k), columns]
                for j in range(1, sub):
                    value = value + part_in_ref[j - 1, rows_of(k), columns].astype(F32)
                summed_ref[i, rows_of(k), :] = value.astype(BF16)
            if not k:
                returned_ref[z * tp + t] = summed_ref[t, rows_of(k), :]

    def give_back(chunk):
        for k in pairs[chunk]:
            for c in range(tp):
                if k or c:
                    return_copy(k, c).start()

    for load in loads[:2]:
        load.wait()
    make_placing(0)
    pl.semaphore_wait(barrier, peers)
    dispatch(0)
    for hop in range(1, hops):
        make_placing(hop)
    for hop in range(hops):
        taking_ref[hop] = placing_ref[hop].T
    for load in loads[2:]:
        load.wait()

    def turn(i, carry):
        columns = pl.ds(pl.multiple_of(i * tile, tile), tile)
        turned_ref[columns, :] = down_ref[0, :, columns].T
        return carry

    lax.fori_loop(0, turned_ref.shape[0] // tile, turn, 0)

    last = chunks - 1

    def own_block():
        arrive(0)
        forward(0)

    def one_hop(hop, carry):
        either(lambda: send(pairs[0][0]), own_block)
        for i in range(1, chunks):
            far, near = pairs[i - 1]
            arrive(far)
            either(lambda: send(pairs[i][0]), lambda: forward(far))
            send(pairs[i][1])
            if i >= 2:
                arrive(near)
                forward(near)
                project(i - 2)
                exchange(i - 2)
            expand(i - 1)
        for k in pairs[last]:
            if k:
                arrive(k)
                forward(k)
        if last:
            project(last - 1)
            exchange(last - 1)
        expand(last)
        for k in range(ep):
            for j in range(1, sub):
                forward_copy(k, j).wait_send()
        for chunk in range(last):
            sum_up(chunk)
        project(last)
        either(lambda: exchange(last), lambda: [give_back(chunk) for chunk in range(last)])
        sum_up(last)
        give_back(last)
        for k, c in remote:
            dispatch_copy(k, c).wait_send()
        for k, c in remote:
            return_copy(k, c).wait_recv()
        update = jnp.dot(
            taking_ref[hop],
            returned_ref[...].reshape(experts * cap, quarter),
            preferred_element_type=F32,
        )
        state_ref[...] = (state_ref[...].astype(F32) + update).astype(BF16)

        @pl.when(hop < hops - 1)
        def _():
            dispatch(hop + 1)

        for k in range(ep):
            for j in range(1, sub):
                part_copy(k, j).wait_send()
        for k, c in remote:
            return_copy(k, c).wait_send()
        return carry

    lax.fori_loop(0, hops, one_hop, 0)


def shards(sizes, rows, path, norm_gain, gate_weight, up_weight, down_weight):
    ep, tp, sub, cap = sizes
    local_rows, quarter = rows.shape
    hops = path.shape[0]
    hid, width = gate_weight.shape[1:]
    half = quarter * tp
    experts = ep * tp
    dma = pltpu.SemaphoreType.DMA
    vmem, any_space = pl.BlockSpec(memory_space=pltpu.VMEM), pl.BlockSpec(memory_space=pl.ANY)
    return pl.pallas_call(
        functools.partial(chain_kernel, sizes),
        out_shape=jax.ShapeDtypeStruct(rows.shape, rows.dtype),
        in_specs=[any_space] * 6,
        out_specs=vmem,
        scratch_shapes=[
            pltpu.VMEM((hops, local_rows), jnp.int32),
            pltpu.VMEM((1, width), F32),
            pltpu.VMEM((1, hid, width), BF16),
            pltpu.VMEM((1, hid, width), BF16),
            pltpu.VMEM((1, hid, width), BF16),
            pltpu.VMEM((width, hid), BF16),
            pltpu.VMEM((hops, experts * cap, local_rows), BF16),
            pltpu.VMEM((hops, local_rows, experts * cap), BF16),
            pltpu.VMEM((experts, cap, quarter), BF16),
            pltpu.VMEM((sub * tp, ep * cap, quarter), BF16),
            pltpu.VMEM((ep * cap, width), BF16),
            pltpu.VMEM((ep // 2, hid, 2 * cap), BF16),
            pltpu.VMEM((sub - 1, ep * cap, half), BF16),
            pltpu.VMEM((sub - 1, ep * cap, half), BF16),
            pltpu.VMEM((ep * cap, half), F32),
            pltpu.VMEM((tp, ep * cap, quarter), BF16),
            pltpu.VMEM((experts, cap, quarter), BF16),
            dma((6,)),
            dma((ep, tp)),
            dma((ep, tp)),
            dma((ep, sub - 1)),
            dma((ep, sub - 1)),
            dma((ep, sub - 1)),
            dma((ep, sub - 1)),
            dma((ep, tp)),
            dma((ep, tp)),
        ],
        compiler_params=pltpu.CompilerParams(
            collective_id=0, has_side_effects=True, vmem_limit_bytes=56 * 1024 * 1024
        ),
        cost_estimate=pl.CostEstimate(
            flops=2 * hops * ep * cap * hid * width * 3,
            bytes_accessed=3 * hid * width * 2,
            transcendentals=hops * ep * cap * hid,
        ),
    )(rows, path[:, :, 0], norm_gain, gate_weight, up_weight, down_weight)


def solution(mesh):
    ep, tp, sub = mesh.shape["ep"], mesh.shape["tp"], mesh.shape["sub"]

    def run(rows, path, norm_gain, gate_weight, up_weight, down_weight):
        cap = max(16, 2 * rows.shape[0] // (ep * tp))
        sizes = (ep, tp, sub, cap)
        return shards(sizes, rows, path, norm_gain, gate_weight, up_weight, down_weight)

    in_specs = (
        P(("groups", "ep"), ("sub", "tp")),
        P(None, ("groups", "ep"), None),
        P(("ep", "tp"), None),
        P(("ep", "tp"), "sub", None),
        P(("ep", "tp"), "sub", None),
        P(("ep", "tp"), "sub", None),
    )
    out_specs = P(("groups", "ep"), ("sub", "tp"))
    return jax.shard_map(run, mesh=mesh, in_specs=in_specs, out_specs=out_specs, check_vma=False)
```

```python
import functools

import jax
import jax.numpy as jnp
from jax import lax
from jax.experimental import pallas as pl
from jax.experimental.pallas import tpu as pltpu
from jax.sharding import PartitionSpec as P

EPS = 1e-06
MESH = pl.DeviceIdType.MESH
F32 = jnp.float32
BF16 = jnp.bfloat16


def partner(index, distance, count):
    out, bit = 0, 1
    while bit < count:
        own = (index // bit) % 2
        out = out + bit * ((1 - own) if (distance // bit) % 2 else own)
        bit *= 2
    return out


def chain_kernel(
    sizes,
    rows_hbm,
    path_hbm,
    gain_hbm,
    gate_hbm,
    up_hbm,
    down_hbm,
    state_ref,
    path_ref,
    gain_ref,
    gate_ref,
    up_ref,
    down_ref,
    turned_ref,
    placing_ref,
    taking_ref,
    packed_ref,
    arrived_ref,
    normed_ref,
    hidden_ref,
    part_out_ref,
    part_in_ref,
    own_ref,
    summed_ref,
    returned_ref,
    load_sem,
    disp_send,
    disp_recv,
    fwd_send,
    fwd_recv,
    part_send,
    part_recv,
    ret_send,
    ret_recv,
):
    ep, tp, sub, cap = sizes
    z, s, t = lax.axis_index("ep"), lax.axis_index("sub"), lax.axis_index("tp")
    hops = path_ref.shape[0]
    local_rows, quarter = state_ref.shape
    half = quarter * tp
    experts = ep * tp
    far, near = list(range(ep // 2, ep)), list(range(1, ep // 2))
    order = far + near + [0]
    here = s * tp + t

    loads = [
        pltpu.make_async_copy(src, dst, load_sem.at[i])
        for i, (src, dst) in enumerate(
            (
                (rows_hbm, state_ref),
                (path_hbm, path_ref),
                (gate_hbm, gate_ref),
                (up_hbm, up_ref),
                (down_hbm, down_ref),
                (gain_hbm, gain_ref),
            )
        )
    ]
    for load in loads:
        load.start()

    barrier = pltpu.get_barrier_semaphore()
    peers = 0
    for k in range(ep):
        for c in range(tp):
            if k or c:
                pl.semaphore_signal(
                    barrier, inc=1,
                    device_id={"ep": partner(z, k, ep), "tp": (t + c) % tp},
                    device_id_type=MESH,
                )
                peers += 1
    for j in range(1, sub):
        pl.semaphore_signal(
            barrier, inc=1, device_id={"sub": (s + j) % sub}, device_id_type=MESH
        )
        peers += 1

    def rows_of(k):
        return pl.ds(order.index(k) * cap, cap)

    def dispatch_copy(k, c):
        to_z, to_t = partner(z, k, ep), (t + c) % tp
        return pltpu.make_async_remote_copy(
            src_ref=packed_ref.at[to_z * tp + to_t],
            dst_ref=arrived_ref.at[here, rows_of(k)],
            send_sem=disp_send.at[k, c],
            recv_sem=disp_recv.at[k, c],
            device_id={"ep": to_z, "tp": to_t},
            device_id_type=MESH,
        )

    def forward_copy(k, c, j):
        block = arrived_ref.at[s * tp + (t + tp - c) % tp, rows_of(k)]
        return pltpu.make_async_remote_copy(
            src_ref=block,
            dst_ref=block,
            send_sem=fwd_send.at[k, c, j - 1],
            recv_sem=fwd_recv.at[k, c, j - 1],
            device_id={"sub": (s + j) % sub},
            device_id_type=MESH,
        )

    def part_copy(k, c, j):
        return pltpu.make_async_remote_copy(
            src_ref=part_out_ref.at[j - 1, c, rows_of(k)],
            dst_ref=part_in_ref.at[j - 1, c, rows_of(k)],
            send_sem=part_send.at[k, c, j - 1],
            recv_sem=part_recv.at[k, c, j - 1],
            device_id={"sub": (s + j) % sub},
            device_id_type=MESH,
        )

    def return_copy(k, c):
        to_z, to_t = partner(z, k, ep), (t + c) % tp
        return pltpu.make_async_remote_copy(
            src_ref=summed_ref.at[c, rows_of(k)],
            dst_ref=returned_ref.at[z * tp + t],
            send_sem=ret_send.at[k, c],
            recv_sem=ret_recv.at[k, c],
            device_id={"ep": to_z, "tp": to_t},
            device_id_type=MESH,
        )

    cores, others = range(tp), range(1, sub)
    remote = [(k, c) for k in order for c in cores if k or c]

    def make_placing(hop):
        named = path_ref[pl.ds(hop, 1), :]
        lines = -(-experts // 8) * 8
        onehot = (
            lax.broadcasted_iota(jnp.int32, (lines, local_rows), 0) == named
        ).astype(F32)
        earlier = (
            lax.broadcasted_iota(jnp.int32, (local_rows, local_rows), 0)
            < lax.broadcasted_iota(jnp.int32, (local_rows, local_rows), 1)
        ).astype(F32)
        before = jnp.dot(
            onehot.astype(BF16), earlier.astype(BF16), preferred_element_type=F32
        )
        rank = jnp.sum(before * onehot, axis=0, keepdims=True)
        target = named.astype(F32) * float(cap) + rank
        slots = lax.broadcasted_iota(jnp.int32, (experts * cap, local_rows), 0)
        placing_ref[hop] = jnp.where(slots.astype(F32) == target, 1.0, 0.0).astype(BF16)

    def dispatch(hop):
        for k in [0] + order[:-1]:
            first = partner(z, k, ep) * tp
            lines = pl.ds(pl.multiple_of(first * cap, 16), tp * cap)
            packed = jnp.dot(
                placing_ref[hop, lines, :], state_ref[...], preferred_element_type=F32
            ).astype(BF16)
            for i in range(tp):
                packed_ref[first + i] = packed[i * cap : (i + 1) * cap]
            for c in range(tp):
                if k or c:
                    dispatch_copy(k, c).start()
                else:
                    arrived_ref[here, rows_of(0), :] = packed_ref[z * tp + t]

    def forward(k):
        for c in cores:
            if k or c:
                dispatch_copy(k, c).wait_recv()
            for j in others:
                forward_copy(k, c, j).start()

    def normalise(k):
        for c in cores:
            for j in others:
                forward_copy(k, c, j).wait_recv()
        total = jnp.zeros((cap, 1), F32)
        for q in range(sub * tp):
            value = arrived_ref[q, rows_of(k), :].astype(F32)
            total = total + jnp.sum(value * value, axis=-1, keepdims=True)
        scale = lax.rsqrt(total / float(quarter * sub * tp) + EPS)
        for q in range(sub * tp):
            value = arrived_ref[q, rows_of(k), :].astype(F32)
            columns = pl.ds(q * quarter, quarter)
            normed_ref[rows_of(k), columns] = (
                value * scale * gain_ref[:, columns]
            ).astype(BF16)

    def expand():
        normed = normed_ref[...]
        dims = (((1,), (1,)), ((), ()))
        gate = lax.dot_general(gate_ref[0], normed, dims, preferred_element_type=F32)
        upward = lax.dot_general(up_ref[0], normed, dims, preferred_element_type=F32)
        hidden_ref[...] = (gate / (1.0 + jnp.exp(-gate)) * upward).astype(BF16)

    tile = min(512, quarter)

    def contract(j, c, out):
        base = ((s + j) % sub) * half + (t + c) % tp * quarter

        def step(i, carry):
            inside = pl.ds(pl.multiple_of(i * tile, tile), tile)
            columns = pl.ds(pl.multiple_of(base + i * tile, tile), tile)
            product = jnp.dot(
                turned_ref[columns, :], hidden_ref[...], preferred_element_type=F32
            )
            out[:, inside] = product.T.astype(out.dtype)
            return carry

        lax.fori_loop(0, quarter // tile, step, 0)

    def give_back(k, c):
        for j in others:
            part_copy(k, c, j).wait_recv()
        value = own_ref[c, rows_of(k), :]
        for j in others:
            value = value + part_in_ref[j - 1, c, rows_of(k), :].astype(F32)
        summed_ref[c, rows_of(k), :] = value.astype(BF16)
        if k or c:
            return_copy(k, c).start()
        else:
            returned_ref[z * tp + t] = summed_ref[0, rows_of(k), :]

    for load in loads[:2]:
        load.wait()
    make_placing(0)
    pl.semaphore_wait(barrier, peers)
    dispatch(0)
    for hop in range(1, hops):
        make_placing(hop)
    for hop in range(hops):
        taking_ref[hop] = placing_ref[hop].T
    for load in loads[2:]:
        load.wait()

    def turn(i, carry):
        columns = pl.ds(pl.multiple_of(i * tile, tile), tile)
        turned_ref[columns, :] = down_ref[0, :, columns].T
        return carry

    lax.fori_loop(0, turned_ref.shape[0] // tile, turn, 0)

    def one_hop(hop, carry):
        forward(0)
        forward(far[0])
        for k, ahead in zip(near, far[1:]):
            forward(k)
            forward(ahead)
        for k in [0] + near + far:
            normalise(k)
        expand()
        for c in cores:
            for j in others:
                contract(j, c, part_out_ref.at[j - 1, c])
                for k in order:
                    part_copy(k, c, j).start()
        for c in cores:
            contract(0, c, own_ref.at[c])
        for k in order:
            for c in cores:
                for j in others:
                    forward_copy(k, c, j).wait_send()
        for c in cores:
            for k in order:
                give_back(k, c)
        for k, c in remote:
            dispatch_copy(k, c).wait_send()
        for k, c in remote:
            return_copy(k, c).wait_recv()
        update = jnp.dot(
            taking_ref[hop],
            returned_ref[...].reshape(experts * cap, quarter),
            preferred_element_type=F32,
        )
        state_ref[...] = (state_ref[...].astype(F32) + update).astype(BF16)

        @pl.when(hop < hops - 1)
        def _():
            dispatch(hop + 1)

        for k in order:
            for c in cores:
                for j in others:
                    part_copy(k, c, j).wait_send()
        for k, c in remote:
            return_copy(k, c).wait_send()
        return carry

    lax.fori_loop(0, hops, one_hop, 0)


def shards(sizes, rows, path, norm_gain, gate_weight, up_weight, down_weight):
    ep, tp, sub, cap = sizes
    local_rows, quarter = rows.shape
    hops = path.shape[0]
    hid, width = gate_weight.shape[1:]
    experts = ep * tp
    dma = pltpu.SemaphoreType.DMA
    vmem, any_space = pl.BlockSpec(memory_space=pltpu.VMEM), pl.BlockSpec(memory_space=pl.ANY)
    return pl.pallas_call(
        functools.partial(chain_kernel, sizes),
        out_shape=jax.ShapeDtypeStruct(rows.shape, rows.dtype),
        in_specs=[any_space] * 6,
        out_specs=vmem,
        scratch_shapes=[
            pltpu.VMEM((hops, local_rows), jnp.int32),
            pltpu.VMEM((1, width), F32),
            pltpu.VMEM((1, hid, width), BF16),
            pltpu.VMEM((1, hid, width), BF16),
            pltpu.VMEM((1, hid, width), BF16),
            pltpu.VMEM((width, hid), BF16),
            pltpu.VMEM((hops, experts * cap, local_rows), BF16),
            pltpu.VMEM((hops, local_rows, experts * cap), BF16),
            pltpu.VMEM((experts, cap, quarter), BF16),
            pltpu.VMEM((sub * tp, ep * cap, quarter), BF16),
            pltpu.VMEM((ep * cap, width), BF16),
            pltpu.VMEM((hid, ep * cap), BF16),
            pltpu.VMEM((sub - 1, tp, ep * cap, quarter), BF16),
            pltpu.VMEM((sub - 1, tp, ep * cap, quarter), BF16),
            pltpu.VMEM((tp, ep * cap, quarter), F32),
            pltpu.VMEM((tp, ep * cap, quarter), BF16),
            pltpu.VMEM((experts, cap, quarter), BF16),
            dma((6,)),
            dma((ep, tp)),
            dma((ep, tp)),
            dma((ep, tp, sub - 1)),
            dma((ep, tp, sub - 1)),
            dma((ep, tp, sub - 1)),
            dma((ep, tp, sub - 1)),
            dma((ep, tp)),
            dma((ep, tp)),
        ],
        compiler_params=pltpu.CompilerParams(
            collective_id=0, has_side_effects=True, vmem_limit_bytes=56 * 1024 * 1024
        ),
        cost_estimate=pl.CostEstimate(
            flops=2 * hops * ep * cap * hid * width * 3,
            bytes_accessed=3 * hid * width * 2,
            transcendentals=hops * ep * cap * hid,
        ),
    )(rows, path[:, :, 0], norm_gain, gate_weight, up_weight, down_weight)


def solution(mesh):
    ep, tp, sub = mesh.shape["ep"], mesh.shape["tp"], mesh.shape["sub"]

    def run(rows, path, norm_gain, gate_weight, up_weight, down_weight):
        cap = max(16, 2 * rows.shape[0] // (ep * tp))
        sizes = (ep, tp, sub, cap)
        return shards(sizes, rows, path, norm_gain, gate_weight, up_weight, down_weight)

    in_specs = (
        P(("groups", "ep"), ("sub", "tp")),
        P(None, ("groups", "ep"), None),
        P(("ep", "tp"), None),
        P(("ep", "tp"), "sub", None),
        P(("ep", "tp"), "sub", None),
        P(("ep", "tp"), "sub", None),
    )
    out_specs = P(("groups", "ep"), ("sub", "tp"))
    return jax.shard_map(run, mesh=mesh, in_specs=in_specs, out_specs=out_specs, check_vma=False)
```

```python
import functools

import jax
import jax.numpy as jnp
from jax import lax
from jax.experimental import pallas as pl
from jax.experimental.pallas import tpu as pltpu
from jax.sharding import PartitionSpec as P

EPS = 1e-06
LANES = 128
MESH = pl.DeviceIdType.MESH
F32 = jnp.float32
BF16 = jnp.bfloat16


def partner(index, distance, count):
    out, bit = 0, 1
    while bit < count:
        own = (index // bit) % 2
        out = out + bit * ((1 - own) if (distance // bit) % 2 else own)
        bit *= 2
    return out


def chain_kernel(
    sizes,
    rows_hbm,
    path_hbm,
    gain_hbm,
    gate_hbm,
    up_hbm,
    down_hbm,
    state_ref,
    path_ref,
    gain_ref,
    gate_ref,
    up_ref,
    down_ref,
    turned_ref,
    placing_ref,
    taking_ref,
    packed_ref,
    arrived_ref,
    normed_ref,
    squares_ref,
    gate_acc,
    up_acc,
    hidden_ref,
    part_out_ref,
    part_in_ref,
    own_ref,
    summed_ref,
    returned_ref,
    load_sem,
    disp_send,
    disp_recv,
    fwd_send,
    fwd_recv,
    part_send,
    part_recv,
    ret_send,
    ret_recv,
):
    ep, tp, sub, cap = sizes
    z, s, t = lax.axis_index("ep"), lax.axis_index("sub"), lax.axis_index("tp")
    hops = path_ref.shape[0]
    local_rows, quarter = state_ref.shape
    half = quarter * tp
    experts = ep * tp
    far, near = list(range(ep // 2, ep)), list(range(1, ep // 2))
    order = far + near + [0]
    here = s * tp + t

    loads = [
        pltpu.make_async_copy(src, dst, load_sem.at[i])
        for i, (src, dst) in enumerate(
            (
                (rows_hbm, state_ref),
                (path_hbm, path_ref),
                (gate_hbm, gate_ref),
                (up_hbm, up_ref),
                (down_hbm, down_ref),
                (gain_hbm, gain_ref),
            )
        )
    ]
    for load in loads:
        load.start()

    barrier = pltpu.get_barrier_semaphore()
    peers = 0
    for k in range(ep):
        for c in range(tp):
            if k or c:
                pl.semaphore_signal(
                    barrier, inc=1,
                    device_id={"ep": partner(z, k, ep), "tp": (t + c) % tp},
                    device_id_type=MESH,
                )
                peers += 1
    for j in range(1, sub):
        pl.semaphore_signal(
            barrier, inc=1, device_id={"sub": (s + j) % sub}, device_id_type=MESH
        )
        peers += 1

    def rows_of(k):
        return pl.ds(order.index(k) * cap, cap)

    def dispatch_copy(k, c):
        to_z, to_t = partner(z, k, ep), (t + c) % tp
        return pltpu.make_async_remote_copy(
            src_ref=packed_ref.at[to_z * tp + to_t],
            dst_ref=arrived_ref.at[here, rows_of(k)],
            send_sem=disp_send.at[k, c],
            recv_sem=disp_recv.at[k, c],
            device_id={"ep": to_z, "tp": to_t},
            device_id_type=MESH,
        )

    def forward_copy(k, c, j):
        block = arrived_ref.at[s * tp + (t + tp - c) % tp, rows_of(k)]
        return pltpu.make_async_remote_copy(
            src_ref=block,
            dst_ref=block,
            send_sem=fwd_send.at[k, c, j - 1],
            recv_sem=fwd_recv.at[k, c, j - 1],
            device_id={"sub": (s + j) % sub},
            device_id_type=MESH,
        )

    def part_copy(k, c, j):
        return pltpu.make_async_remote_copy(
            src_ref=part_out_ref.at[j - 1, c, rows_of(k)],
            dst_ref=part_in_ref.at[j - 1, c, rows_of(k)],
            send_sem=part_send.at[k, c, j - 1],
            recv_sem=part_recv.at[k, c, j - 1],
            device_id={"sub": (s + j) % sub},
            device_id_type=MESH,
        )

    def return_copy(k, c):
        to_z, to_t = partner(z, k, ep), (t + c) % tp
        return pltpu.make_async_remote_copy(
            src_ref=summed_ref.at[c, rows_of(k)],
            dst_ref=returned_ref.at[z * tp + t],
            send_sem=ret_send.at[k, c],
            recv_sem=ret_recv.at[k, c],
            device_id={"ep": to_z, "tp": to_t},
            device_id_type=MESH,
        )

    cores, others = range(tp), range(1, sub)
    remote = [(k, c) for k in order for c in cores if k or c]

    def make_placing(hop):
        named = path_ref[pl.ds(hop, 1), :]
        lines = -(-experts // 8) * 8
        onehot = (
            lax.broadcasted_iota(jnp.int32, (lines, local_rows), 0) == named
        ).astype(F32)
        earlier = (
            lax.broadcasted_iota(jnp.int32, (local_rows, local_rows), 0)
            < lax.broadcasted_iota(jnp.int32, (local_rows, local_rows), 1)
        ).astype(F32)
        before = jnp.dot(
            onehot.astype(BF16), earlier.astype(BF16), preferred_element_type=F32
        )
        rank = jnp.sum(before * onehot, axis=0, keepdims=True)
        target = named.astype(F32) * float(cap) + rank
        slots = lax.broadcasted_iota(jnp.int32, (experts * cap, local_rows), 0)
        placing_ref[hop] = jnp.where(slots.astype(F32) == target, 1.0, 0.0).astype(BF16)

    def dispatch(hop):
        for k in [0] + order[:-1]:
            first = partner(z, k, ep) * tp
            lines = pl.ds(pl.multiple_of(first * cap, 16), tp * cap)
            packed = jnp.dot(
                placing_ref[hop, lines, :], state_ref[...], preferred_element_type=F32
            ).astype(BF16)
            for i in range(tp):
                packed_ref[first + i] = packed[i * cap : (i + 1) * cap]
            for c in range(tp):
                if k or c:
                    dispatch_copy(k, c).start()
                else:
                    arrived_ref[here, rows_of(0), :] = packed_ref[z * tp + t]

    def forward(k):
        for c in cores:
            if k or c:
                dispatch_copy(k, c).wait_recv()
            for j in others:
                forward_copy(k, c, j).start()

    def weigh(k, j):
        section = (s + sub - j) % sub
        squares = jnp.zeros((cap, LANES), F32)
        for i in cores:
            q = section * tp + i
            value = arrived_ref[q, rows_of(k), :].astype(F32)
            for lane in range(0, quarter, LANES):
                piece = value[:, lane : lane + LANES]
                squares = squares + piece * piece
            columns = pl.ds(pl.multiple_of(q * quarter, LANES), quarter)
            normed_ref[j, rows_of(k), pl.ds(i * quarter, quarter)] = (
                value * gain_ref[:, columns]
            ).astype(BF16)
        if j:
            squares = squares + squares_ref[rows_of(k), :]
        squares_ref[rows_of(k), :] = squares

    def expand():
        dims = (((1,), (1,)), ((), ()))
        for j in range(sub):
            if j:
                for k in order:
                    for c in cores:
                        forward_copy(k, c, j).wait_recv()
            for k in order:
                weigh(k, j)
            section = (s + sub - j) % sub
            columns = pl.ds(pl.multiple_of(section * half, LANES), half)
            for acc, weight_ref in ((gate_acc, gate_ref), (up_acc, up_ref)):
                product = lax.dot_general(
                    weight_ref[0, :, columns], normed_ref[j], dims, preferred_element_type=F32
                )
                acc[...] = acc[...] + product if j else product
        total = jnp.sum(squares_ref[...].T, axis=0, keepdims=True)
        scale = lax.rsqrt(total / float(half * sub) + EPS)
        gate, upward = gate_acc[...] * scale, up_acc[...] * scale
        hidden_ref[...] = (gate / (1.0 + jnp.exp(-gate)) * upward).astype(BF16)

    tile = min(512, quarter)

    def contract(j, c, out):
        base = ((s + j) % sub) * half + (t + c) % tp * quarter

        def step(i, carry):
            inside = pl.ds(pl.multiple_of(i * tile, tile), tile)
            columns = pl.ds(pl.multiple_of(base + i * tile, tile), tile)
            product = jnp.dot(
                turned_ref[columns, :], hidden_ref[...], preferred_element_type=F32
            )
            out[:, inside] = product.T.astype(out.dtype)
            return carry

        lax.fori_loop(0, quarter // tile, step, 0)

    def give_back(k, c):
        for j in others:
            part_copy(k, c, j).wait_recv()
        value = own_ref[c, rows_of(k), :]
        for j in others:
            value = value + part_in_ref[j - 1, c, rows_of(k), :].astype(F32)
        summed_ref[c, rows_of(k), :] = value.astype(BF16)
        if k or c:
            return_copy(k, c).start()
        else:
            returned_ref[z * tp + t] = summed_ref[0, rows_of(k), :]

    for load in loads[:2]:
        load.wait()
    make_placing(0)
    pl.semaphore_wait(barrier, peers)
    dispatch(0)
    for hop in range(1, hops):
        make_placing(hop)
    for hop in range(hops):
        taking_ref[hop] = placing_ref[hop].T
    for load in loads[2:]:
        load.wait()

    def turn(i, carry):
        columns = pl.ds(pl.multiple_of(i * tile, tile), tile)
        turned_ref[columns, :] = down_ref[0, :, columns].T
        return carry

    lax.fori_loop(0, turned_ref.shape[0] // tile, turn, 0)

    def one_hop(hop, carry):
        forward(0)
        forward(far[0])
        for k, ahead in zip(near, far[1:]):
            forward(k)
            forward(ahead)
        expand()
        for c in cores:
            for j in others:
                contract(j, c, part_out_ref.at[j - 1, c])
                for k in order:
                    part_copy(k, c, j).start()
        for c in cores:
            contract(0, c, own_ref.at[c])
        for k in order:
            for c in cores:
                for j in others:
                    forward_copy(k, c, j).wait_send()
        for c in cores:
            for k in order:
                give_back(k, c)
        for k, c in remote:
            dispatch_copy(k, c).wait_send()
        for k, c in remote:
            return_copy(k, c).wait_recv()
        update = jnp.dot(
            taking_ref[hop],
            returned_ref[...].reshape(experts * cap, quarter),
            preferred_element_type=F32,
        )
        state_ref[...] = (state_ref[...].astype(F32) + update).astype(BF16)

        @pl.when(hop < hops - 1)
        def _():
            dispatch(hop + 1)

        for k in order:
            for c in cores:
                for j in others:
                    part_copy(k, c, j).wait_send()
        for k, c in remote:
            return_copy(k, c).wait_send()
        return carry

    lax.fori_loop(0, hops, one_hop, 0)


def shards(sizes, rows, path, norm_gain, gate_weight, up_weight, down_weight):
    ep, tp, sub, cap = sizes
    local_rows, quarter = rows.shape
    hops = path.shape[0]
    hid, width = gate_weight.shape[1:]
    experts = ep * tp
    dma = pltpu.SemaphoreType.DMA
    vmem, any_space = pl.BlockSpec(memory_space=pltpu.VMEM), pl.BlockSpec(memory_space=pl.ANY)
    return pl.pallas_call(
        functools.partial(chain_kernel, sizes),
        out_shape=jax.ShapeDtypeStruct(rows.shape, rows.dtype),
        in_specs=[any_space] * 6,
        out_specs=vmem,
        scratch_shapes=[
            pltpu.VMEM((hops, local_rows), jnp.int32),
            pltpu.VMEM((1, width), F32),
            pltpu.VMEM((1, hid, width), BF16),
            pltpu.VMEM((1, hid, width), BF16),
            pltpu.VMEM((1, hid, width), BF16),
            pltpu.VMEM((width, hid), BF16),
            pltpu.VMEM((hops, experts * cap, local_rows), BF16),
            pltpu.VMEM((hops, local_rows, experts * cap), BF16),
            pltpu.VMEM((experts, cap, quarter), BF16),
            pltpu.VMEM((sub * tp, ep * cap, quarter), BF16),
            pltpu.VMEM((sub, ep * cap, width // sub), BF16),
            pltpu.VMEM((ep * cap, LANES), F32),
            pltpu.VMEM((hid, ep * cap), F32),
            pltpu.VMEM((hid, ep * cap), F32),
            pltpu.VMEM((hid, ep * cap), BF16),
            pltpu.VMEM((sub - 1, tp, ep * cap, quarter), BF16),
            pltpu.VMEM((sub - 1, tp, ep * cap, quarter), BF16),
            pltpu.VMEM((tp, ep * cap, quarter), F32),
            pltpu.VMEM((tp, ep * cap, quarter), BF16),
            pltpu.VMEM((experts, cap, quarter), BF16),
            dma((6,)),
            dma((ep, tp)),
            dma((ep, tp)),
            dma((ep, tp, sub - 1)),
            dma((ep, tp, sub - 1)),
            dma((ep, tp, sub - 1)),
            dma((ep, tp, sub - 1)),
            dma((ep, tp)),
            dma((ep, tp)),
        ],
        compiler_params=pltpu.CompilerParams(
            collective_id=0, has_side_effects=True, vmem_limit_bytes=56 * 1024 * 1024
        ),
        cost_estimate=pl.CostEstimate(
            flops=2 * hops * ep * cap * hid * width * 3,
            bytes_accessed=3 * hid * width * 2,
            transcendentals=hops * ep * cap * hid,
        ),
    )(rows, path[:, :, 0], norm_gain, gate_weight, up_weight, down_weight)


def solution(mesh):
    ep, tp, sub = mesh.shape["ep"], mesh.shape["tp"], mesh.shape["sub"]

    def run(rows, path, norm_gain, gate_weight, up_weight, down_weight):
        cap = max(16, 2 * rows.shape[0] // (ep * tp))
        sizes = (ep, tp, sub, cap)
        return shards(sizes, rows, path, norm_gain, gate_weight, up_weight, down_weight)

    in_specs = (
        P(("groups", "ep"), ("sub", "tp")),
        P(None, ("groups", "ep"), None),
        P(("ep", "tp"), None),
        P(("ep", "tp"), "sub", None),
        P(("ep", "tp"), "sub", None),
        P(("ep", "tp"), "sub", None),
    )
    out_specs = P(("groups", "ep"), ("sub", "tp"))
    return jax.shard_map(run, mesh=mesh, in_specs=in_specs, out_specs=out_specs, check_vma=False)
```

```python
import functools

import jax
import jax.numpy as jnp
from jax import lax
from jax.experimental import pallas as pl
from jax.experimental.pallas import tpu as pltpu
from jax.sharding import PartitionSpec as P

EPS = 1e-06
LANES = 128
MESH = pl.DeviceIdType.MESH
F32 = jnp.float32
BF16 = jnp.bfloat16


def partner(index, distance, count):
    out, bit = 0, 1
    while bit < count:
        own = (index // bit) % 2
        out = out + bit * ((1 - own) if (distance // bit) % 2 else own)
        bit *= 2
    return out


def chain_kernel(
    sizes,
    rows_hbm,
    path_hbm,
    gain_hbm,
    gate_hbm,
    up_hbm,
    down_hbm,
    state_ref,
    path_ref,
    gain_ref,
    gate_ref,
    up_ref,
    down_ref,
    turned_ref,
    placing_ref,
    taking_ref,
    packed_ref,
    arrived_ref,
    normed_ref,
    squares_ref,
    gate_acc,
    up_acc,
    hidden_ref,
    part_out_ref,
    part_in_ref,
    own_ref,
    summed_ref,
    returned_ref,
    load_sem,
    disp_send,
    disp_recv,
    fwd_send,
    fwd_recv,
    part_send,
    part_recv,
    ret_send,
    ret_recv,
):
    ep, tp, sub, cap = sizes
    z, s, t = lax.axis_index("ep"), lax.axis_index("sub"), lax.axis_index("tp")
    hops = path_ref.shape[0]
    local_rows, quarter = state_ref.shape
    half = quarter * tp
    experts = ep * tp
    far, near = list(range(ep // 2, ep)), list(range(1, ep // 2))
    order = far + near + [0]
    coming = [k for pair in zip([0] + near, far) for k in pair]
    here = s * tp + t

    loads = [
        pltpu.make_async_copy(src, dst, load_sem.at[i])
        for i, (src, dst) in enumerate(
            (
                (rows_hbm, state_ref),
                (path_hbm, path_ref),
                (gate_hbm, gate_ref),
                (up_hbm, up_ref),
                (down_hbm, down_ref),
                (gain_hbm, gain_ref),
            )
        )
    ]
    for load in loads:
        load.start()

    barrier = pltpu.get_barrier_semaphore()
    peers = 0
    for k in range(ep):
        for c in range(tp):
            if k or c:
                pl.semaphore_signal(
                    barrier, inc=1,
                    device_id={"ep": partner(z, k, ep), "tp": (t + c) % tp},
                    device_id_type=MESH,
                )
                peers += 1
    for j in range(1, sub):
        pl.semaphore_signal(
            barrier, inc=1, device_id={"sub": (s + j) % sub}, device_id_type=MESH
        )
        peers += 1

    def rows_of(k):
        return pl.ds(order.index(k) * cap, cap)

    def dispatch_copy(k, c):
        to_z, to_t = partner(z, k, ep), (t + c) % tp
        return pltpu.make_async_remote_copy(
            src_ref=packed_ref.at[to_z * tp + to_t],
            dst_ref=arrived_ref.at[here, rows_of(k)],
            send_sem=disp_send.at[k, c],
            recv_sem=disp_recv.at[k, c],
            device_id={"ep": to_z, "tp": to_t},
            device_id_type=MESH,
        )

    def forward_copy(k, c, j):
        block = arrived_ref.at[s * tp + (t + tp - c) % tp, rows_of(k)]
        return pltpu.make_async_remote_copy(
            src_ref=block,
            dst_ref=block,
            send_sem=fwd_send.at[k, c, j - 1],
            recv_sem=fwd_recv.at[k, c, j - 1],
            device_id={"sub": (s + j) % sub},
            device_id_type=MESH,
        )

    def part_copy(k, c, j):
        return pltpu.make_async_remote_copy(
            src_ref=part_out_ref.at[j - 1, c, rows_of(k)],
            dst_ref=part_in_ref.at[j - 1, c, rows_of(k)],
            send_sem=part_send.at[k, c, j - 1],
            recv_sem=part_recv.at[k, c, j - 1],
            device_id={"sub": (s + j) % sub},
            device_id_type=MESH,
        )

    def return_copy(k, c):
        to_z, to_t = partner(z, k, ep), (t + c) % tp
        return pltpu.make_async_remote_copy(
            src_ref=summed_ref.at[c, rows_of(k)],
            dst_ref=returned_ref.at[z * tp + t],
            send_sem=ret_send.at[k, c],
            recv_sem=ret_recv.at[k, c],
            device_id={"ep": to_z, "tp": to_t},
            device_id_type=MESH,
        )

    cores, others = range(tp), range(1, sub)
    remote = [(k, c) for k in order for c in cores if k or c]

    def make_placing(hop):
        named = path_ref[pl.ds(hop, 1), :]
        lines = -(-experts // 8) * 8
        onehot = (
            lax.broadcasted_iota(jnp.int32, (lines, local_rows), 0) == named
        ).astype(F32)
        earlier = (
            lax.broadcasted_iota(jnp.int32, (local_rows, local_rows), 0)
            < lax.broadcasted_iota(jnp.int32, (local_rows, local_rows), 1)
        ).astype(F32)
        before = jnp.dot(
            onehot.astype(BF16), earlier.astype(BF16), preferred_element_type=F32
        )
        rank = jnp.sum(before * onehot, axis=0, keepdims=True)
        target = named.astype(F32) * float(cap) + rank
        slots = lax.broadcasted_iota(jnp.int32, (experts * cap, local_rows), 0)
        placing_ref[hop] = jnp.where(slots.astype(F32) == target, 1.0, 0.0).astype(BF16)

    def dispatch(hop):
        line = ep // 2
        for blocks, side in ((far, 1 - z // line), ([0] + near, z // line)):
            first = side * line * tp
            lines = pl.ds(pl.multiple_of(first * cap, 16), line * tp * cap)
            packed = jnp.dot(
                placing_ref[hop, lines, :], state_ref[...], preferred_element_type=F32
            ).astype(BF16)
            for i in range(line * tp):
                packed_ref[first + i] = packed[i * cap : (i + 1) * cap]
            for k in blocks:
                for c in cores:
                    if k or c:
                        dispatch_copy(k, c).start()
        arrived_ref[here, rows_of(0), :] = packed_ref[z * tp + t]

    def forward(k):
        for c in cores:
            if k or c:
                dispatch_copy(k, c).wait_recv()
            for j in others:
                forward_copy(k, c, j).start()
        weigh(k, 0)

    def weigh(k, j):
        section = (s + sub - j) % sub
        squares = jnp.zeros((cap, LANES), F32)
        for i in cores:
            q = section * tp + i
            value = arrived_ref[q, rows_of(k), :].astype(F32)
            for lane in range(0, quarter, LANES):
                piece = value[:, lane : lane + LANES]
                squares = squares + piece * piece
            columns = pl.ds(pl.multiple_of(q * quarter, LANES), quarter)
            normed_ref[j, rows_of(k), pl.ds(i * quarter, quarter)] = (
                value * gain_ref[:, columns]
            ).astype(BF16)
        if j:
            squares = squares + squares_ref[rows_of(k), :]
        squares_ref[rows_of(k), :] = squares

    def expand():
        dims = (((1,), (1,)), ((), ()))
        for j in range(sub):
            for k in coming if j else ():
                for c in cores:
                    forward_copy(k, c, j).wait_recv()
                weigh(k, j)
            section = (s + sub - j) % sub
            columns = pl.ds(pl.multiple_of(section * half, LANES), half)
            for acc, weight_ref in ((gate_acc, gate_ref), (up_acc, up_ref)):
                product = lax.dot_general(
                    weight_ref[0, :, columns], normed_ref[j], dims, preferred_element_type=F32
                )
                acc[...] = acc[...] + product if j else product
        total = jnp.sum(squares_ref[...].T, axis=0, keepdims=True)
        scale = lax.rsqrt(total / float(half * sub) + EPS)
        gate, upward = gate_acc[...] * scale, up_acc[...] * scale
        hidden_ref[...] = (gate / (1.0 + jnp.exp(-gate)) * upward).astype(BF16)

    tile = min(512, quarter)

    def contract(j, c, out):
        base = ((s + j) % sub) * half + (t + c) % tp * quarter

        def step(i, carry):
            inside = pl.ds(pl.multiple_of(i * tile, tile), tile)
            columns = pl.ds(pl.multiple_of(base + i * tile, tile), tile)
            product = jnp.dot(
                turned_ref[columns, :], hidden_ref[...], preferred_element_type=F32
            )
            out[:, inside] = product.T.astype(out.dtype)
            return carry

        lax.fori_loop(0, quarter // tile, step, 0)

    def give_back(k, c):
        for j in others:
            part_copy(k, c, j).wait_recv()
        value = own_ref[c, rows_of(k), :]
        for j in others:
            value = value + part_in_ref[j - 1, c, rows_of(k), :].astype(F32)
        summed_ref[c, rows_of(k), :] = value.astype(BF16)
        if k or c:
            return_copy(k, c).start()
        else:
            returned_ref[z * tp + t] = summed_ref[0, rows_of(k), :]

    for load in loads[:2]:
        load.wait()
    make_placing(0)
    pl.semaphore_wait(barrier, peers)
    dispatch(0)
    for hop in range(1, hops):
        make_placing(hop)
    for hop in range(hops):
        taking_ref[hop] = placing_ref[hop].T
    for load in loads[2:]:
        load.wait()

    def turn(i, carry):
        columns = pl.ds(pl.multiple_of(i * tile, tile), tile)
        turned_ref[columns, :] = down_ref[0, :, columns].T
        return carry

    lax.fori_loop(0, turned_ref.shape[0] // tile, turn, 0)

    def one_hop(hop, carry):
        for k in coming:
            forward(k)
        expand()
        for c in cores:
            for j in others:
                contract(j, c, part_out_ref.at[j - 1, c])
                for k in order:
                    part_copy(k, c, j).start()
        for c in cores:
            contract(0, c, own_ref.at[c])
        for k in order:
            for c in cores:
                for j in others:
                    forward_copy(k, c, j).wait_send()
        for c in cores:
            for k in order:
                give_back(k, c)
        for k, c in remote:
            dispatch_copy(k, c).wait_send()
        for k, c in remote:
            return_copy(k, c).wait_recv()
        update = jnp.dot(
            taking_ref[hop],
            returned_ref[...].reshape(experts * cap, quarter),
            preferred_element_type=F32,
        )
        state_ref[...] = (state_ref[...].astype(F32) + update).astype(BF16)

        @pl.when(hop < hops - 1)
        def _():
            dispatch(hop + 1)

        for k in order:
            for c in cores:
                for j in others:
                    part_copy(k, c, j).wait_send()
        for k, c in remote:
            return_copy(k, c).wait_send()
        return carry

    lax.fori_loop(0, hops, one_hop, 0)


def shards(sizes, rows, path, norm_gain, gate_weight, up_weight, down_weight):
    ep, tp, sub, cap = sizes
    local_rows, quarter = rows.shape
    hops = path.shape[0]
    hid, width = gate_weight.shape[1:]
    experts = ep * tp
    dma = pltpu.SemaphoreType.DMA
    vmem, any_space = pl.BlockSpec(memory_space=pltpu.VMEM), pl.BlockSpec(memory_space=pl.ANY)
    return pl.pallas_call(
        functools.partial(chain_kernel, sizes),
        out_shape=jax.ShapeDtypeStruct(rows.shape, rows.dtype),
        in_specs=[any_space] * 6,
        out_specs=vmem,
        scratch_shapes=[
            pltpu.VMEM((hops, local_rows), jnp.int32),
            pltpu.VMEM((1, width), F32),
            pltpu.VMEM((1, hid, width), BF16),
            pltpu.VMEM((1, hid, width), BF16),
            pltpu.VMEM((1, hid, width), BF16),
            pltpu.VMEM((width, hid), BF16),
            pltpu.VMEM((hops, experts * cap, local_rows), BF16),
            pltpu.VMEM((hops, local_rows, experts * cap), BF16),
            pltpu.VMEM((experts, cap, quarter), BF16),
            pltpu.VMEM((sub * tp, ep * cap, quarter), BF16),
            pltpu.VMEM((sub, ep * cap, width // sub), BF16),
            pltpu.VMEM((ep * cap, LANES), F32),
            pltpu.VMEM((hid, ep * cap), F32),
            pltpu.VMEM((hid, ep * cap), F32),
            pltpu.VMEM((hid, ep * cap), BF16),
            pltpu.VMEM((sub - 1, tp, ep * cap, quarter), BF16),
            pltpu.VMEM((sub - 1, tp, ep * cap, quarter), BF16),
            pltpu.VMEM((tp, ep * cap, quarter), F32),
            pltpu.VMEM((tp, ep * cap, quarter), BF16),
            pltpu.VMEM((experts, cap, quarter), BF16),
            dma((6,)),
            dma((ep, tp)),
            dma((ep, tp)),
            dma((ep, tp, sub - 1)),
            dma((ep, tp, sub - 1)),
            dma((ep, tp, sub - 1)),
            dma((ep, tp, sub - 1)),
            dma((ep, tp)),
            dma((ep, tp)),
        ],
        compiler_params=pltpu.CompilerParams(
            collective_id=0, has_side_effects=True, vmem_limit_bytes=56 * 1024 * 1024
        ),
        cost_estimate=pl.CostEstimate(
            flops=2 * hops * ep * cap * hid * width * 3,
            bytes_accessed=3 * hid * width * 2,
            transcendentals=hops * ep * cap * hid,
        ),
    )(rows, path[:, :, 0], norm_gain, gate_weight, up_weight, down_weight)


def solution(mesh):
    ep, tp, sub = mesh.shape["ep"], mesh.shape["tp"], mesh.shape["sub"]

    def run(rows, path, norm_gain, gate_weight, up_weight, down_weight):
        cap = max(16, 2 * rows.shape[0] // (ep * tp))
        sizes = (ep, tp, sub, cap)
        return shards(sizes, rows, path, norm_gain, gate_weight, up_weight, down_weight)

    in_specs = (
        P(("groups", "ep"), ("sub", "tp")),
        P(None, ("groups", "ep"), None),
        P(("ep", "tp"), None),
        P(("ep", "tp"), "sub", None),
        P(("ep", "tp"), "sub", None),
        P(("ep", "tp"), "sub", None),
    )
    out_specs = P(("groups", "ep"), ("sub", "tp"))
    return jax.shard_map(run, mesh=mesh, in_specs=in_specs, out_specs=out_specs, check_vma=False)
```
